32 devices in a mesh: tm: 8 (over y, x, core), blk: 4 (over z).
Axes of the slice: x: 2, y: 2, z: 4, core: 2. Of those that a mesh axis runs over, the one named last changes fastest.
Arguments:
- dynamics: float32 [256, 256], replicated
- dynamics_mask: int32 [8, 8], replicated, may hold values from 0 to 1, as said below
- obs_op: float32 [256, 256], replicated, may hold values from -0.375 to 0.375
- obs_mask: int32 [8, 8], replicated, may hold values from 0 to 1, as said below
- process_noise: float32 [256], replicated, may hold values from 0.0005 to 0.005
- initial_expectation: float32 [256], replicated, may hold values from -6 to 6
- filter_gains: float32 [128, 256, 256], P('tm', 'blk'), may hold values from -0.01953125 to 0.01953125
- observations: float32 [128, 256], P('tm'), may hold values from -6 to 6
- smooth_gains: float32 [128, 256, 256], P('tm', 'blk')
- filt_cov: float32 [128, 256, 256], P('tm', 'blk')
Outputs:
- smoothed_means: float32 [128, 256], P('tm', 'blk')
- smoothed_cov: float32 [128, 256, 256], P('tm', 'blk')
The draws below stay inside these ranges and needn't reach their ends.
Inputs may be any that keep to these rules, and one draw needn't show every extreme that they name: `dynamics_mask`: diagonal blocks are 1. `obs_mask`: blocks with equal row and column index are 1.
All inputs are finite; a program needn't handle non-finite values.
Results may differ from the reference program's by a relative error of at most 0.0003.
Values sent between devices are 32-bit elements; how exact they have to be, the bound alone decides.
No kernel may reach another device: no remote copies, remote signals or barrier semaphores. Data moves between devices by JAX's collectives and lax.ppermute only.
A program may use at most 256 MiB of HBM per device.

```python
import math
import jax
import jax.numpy as jnp
from jax import lax

S = 256
OBS = 256
NBLK = 8
OBLK = 8
HORIZON_LENGTH = 128


def draw_dynamics(key, part):
    frequency_seed, displacement_seed = jax.random.split(key)
    rates = jnp.exp(jax.random.uniform(frequency_seed, (S,), jnp.float32, jnp.log(0.5 / HORIZON_LENGTH), jnp.log(0.05)))
    coupling = jax.random.normal(displacement_seed, (S, S), jnp.float32) * (0.25 / (S * HORIZON_LENGTH) ** 0.5)
    return jnp.diag(jnp.exp(-rates)) + coupling - coupling.T


def draw_dynamics_mask(key, part):
    pattern = jax.random.randint(jax.random.fold_in(key, 101), (NBLK, NBLK), 0, 2, jnp.int32)
    return jnp.maximum(pattern, jnp.eye(NBLK, dtype=jnp.int32))


def draw_obs_mask(key, part):
    pattern = jax.random.randint(jax.random.fold_in(key, 202), (OBLK, NBLK), 0, 2, jnp.int32)
    return jnp.maximum(pattern, jnp.eye(OBLK, NBLK, dtype=jnp.int32))


def draw_smooth_gains(key, part):
    frequency_seed, displacement_seed, spike_seed = jax.random.split(key, 3)
    rates = jnp.exp(jax.random.uniform(frequency_seed, (S,), jnp.float32, jnp.log(0.5 / HORIZON_LENGTH), jnp.log(0.05)))
    spike_instant = jax.random.randint(spike_seed, (4,), 0, HORIZON_LENGTH, jnp.int32)
    zeroed_elements = jnp.any(jnp.arange(HORIZON_LENGTH)[:, None] == spike_instant[None, :], axis=1)
    level = jnp.where(zeroed_elements, 0.6, 1.0).astype(jnp.float32)
    coupling = jax.random.normal(displacement_seed, (HORIZON_LENGTH, S, S), jnp.float32) * (0.5 / (S * HORIZON_LENGTH) ** 0.5)
    diagonal_entries = jnp.eye(S, dtype=jnp.float32)[None] * (level[:, None, None] * jnp.exp(-rates)[None, None, :])
    return diagonal_entries + coupling - jnp.swapaxes(coupling, 1, 2)


def draw_filt_cov(key, part):
    key_diag, displacement_seed = jax.random.split(key)
    scales = jnp.exp(jax.random.uniform(key_diag, (HORIZON_LENGTH, S), jnp.float32, jnp.log(0.3), jnp.log(3.0)))
    coupling = jax.random.normal(displacement_seed, (HORIZON_LENGTH, S, S), jnp.float32) * 0.014
    diagonal_entries = jnp.eye(S, dtype=jnp.float32)[None] * scales[:, None, :]
    return diagonal_entries + coupling + jnp.swapaxes(coupling, 1, 2)


def block_scale(own_key, extent, cuts, smallest, top_value):
    def one(position, parts):
        draws = jax.random.uniform(jax.random.fold_in(jax.random.fold_in(own_key, 6), position), (parts,), jnp.float32, smallest / len(cuts), top_value / len(cuts))
        return jnp.repeat(jnp.exp(draws), extent[position] // parts).reshape((-1,) + (1,) * (len(extent) - position - 1))

    gain = one(*cuts[0])
    for cut in cuts[1:]:
        gain = gain * one(*cut)
    return gain


def scatter_about(stream_key, shape, spread, limit, cuts=(), kind=jnp.bfloat16):
    result = jax.random.normal(stream_key, shape, jnp.float32) * spread
    if len(cuts) > 0:
        result = block_scale(stream_key, shape, cuts, -0.22, 0.18) * result
    return jnp.clip(result, min=-limit, max=limit).astype(kind)


def setup_inputs(seed: int = 0) -> dict:
    streams_of = jax.random.split(jax.random.key(seed), 11)
    dynamics = draw_dynamics(jax.random.fold_in(streams_of[10], 71), 0)
    dynamics_mask = draw_dynamics_mask(jax.random.fold_in(streams_of[10], 71), 0)
    obs_op = scatter_about(streams_of[2], (OBS, S), S ** -0.5, 0.375, (), jnp.float32)
    obs_mask = draw_obs_mask(jax.random.fold_in(streams_of[10], 71), 0)
    process_noise = jnp.clip(jnp.exp(jax.random.uniform(streams_of[4], (S,), jnp.float32, math.log(0.0005), math.log(0.005))), 0.0005, 0.005)
    initial_expectation = scatter_about(streams_of[5], (S,), 1.0, 6.0, (), jnp.float32)
    filter_gains = scatter_about(streams_of[6], (HORIZON_LENGTH, S, OBS), (HORIZON_LENGTH * 625) ** -0.5, 0.01953125, ((0, 8), (1, 4)), jnp.float32)
    observations = scatter_about(streams_of[7], (HORIZON_LENGTH, OBS), 1.0, 6.0, ((0, 8),), jnp.float32)
    smooth_gains = draw_smooth_gains(jax.random.fold_in(streams_of[10], 71), 0)
    filt_cov = draw_filt_cov(jax.random.fold_in(streams_of[10], 71), 0)
    return {"dynamics": dynamics, "dynamics_mask": dynamics_mask, "obs_op": obs_op, "obs_mask": obs_mask, "process_noise": process_noise, "initial_expectation": initial_expectation, "filter_gains": filter_gains, "observations": observations, "smooth_gains": smooth_gains, "filt_cov": filt_cov}


highest = lax.Precision.HIGHEST


def expand_mask(mask, row_total, col_total):
    row_block = row_total // mask.shape[0]
    col_block = col_total // mask.shape[1]
    return jnp.repeat(jnp.repeat(mask.astype(jnp.float32), row_block, axis=0), col_block, axis=1)


def reference(dynamics, dynamics_mask, obs_op, obs_mask, process_noise, initial_expectation, filter_gains, observations, smooth_gains, filt_cov):
    trans_map = dynamics * expand_mask(dynamics_mask, S, S)
    obs_map = obs_op * expand_mask(obs_mask, OBS, S)
    obs_dyn = jnp.dot(obs_map, trans_map, precision=highest)

    def filter_step(current, inputs):
        gain_now, seen_now = inputs
        step_map = trans_map - jnp.dot(gain_now, obs_dyn, precision=highest)
        step_shift = jnp.dot(gain_now, seen_now, precision=highest)
        current = jnp.dot(step_map, current, precision=highest) + step_shift
        return current, current

    filt_means = lax.scan(filter_step, initial_expectation, (filter_gains, observations))[1]
    final_step = jnp.arange(HORIZON_LENGTH) == HORIZON_LENGTH - 1
    gain_all = jnp.where(final_step[:, None, None], jnp.float32(0.0), smooth_gains)

    def smooth_step(current, inputs):
        cov_next, mean_next = current
        gain_now, cov_filt, mean_filt = inputs
        predicted = jnp.dot(jnp.dot(trans_map, cov_filt, precision=highest), trans_map.T, precision=highest) + jnp.diag(process_noise)
        residual = cov_filt - jnp.dot(jnp.dot(gain_now, predicted, precision=highest), gain_now.T, precision=highest)
        offset = mean_filt - jnp.dot(gain_now, jnp.dot(trans_map, mean_filt, precision=highest), precision=highest)
        cov_now = jnp.dot(jnp.dot(gain_now, cov_next, precision=highest), gain_now.T, precision=highest) + residual
        current_mean = jnp.dot(gain_now, mean_next, precision=highest) + offset
        return (cov_now, current_mean), (current_mean, cov_now)

    start_state = (jnp.zeros((S, S), jnp.float32), jnp.zeros((S,), jnp.float32))
    results = lax.scan(smooth_step, start_state, (gain_all, filt_cov, filt_means), reverse=True)[1]
    return results[0], results[1]
```

```python
import functools

import jax
import jax.numpy as jnp
from jax import lax
from jax.experimental import pallas as pl
from jax.experimental.pallas import tpu as pltpu
from jax.sharding import PartitionSpec as P

highest = lax.Precision.HIGHEST
BOTH = ("tm", "blk")
PAD = 16


def halves(x):
    top = x.astype(jnp.bfloat16)
    return top, (x - top.astype(jnp.float32)).astype(jnp.bfloat16)


def product(left, right, dims):
    def one(a, b):
        return lax.dot_general(a, b, (dims, ((), ())), preferred_element_type=jnp.float32)

    return one(left[0], right[0]) + (one(left[0], right[1]) + one(left[1], right[0]))


def mm(left, right):
    return product(halves(left), halves(right), ((1,), (0,)))


def mm_nt(left, right):
    return product(halves(left), halves(right), ((1,), (1,)))


def rows_of(vec):
    return jnp.broadcast_to(vec, (PAD, vec.shape[-1]))


def expand_mask(mask, row_total, col_total):
    row_block = row_total // mask.shape[0]
    col_block = col_total // mask.shape[1]
    return jnp.repeat(jnp.repeat(mask.astype(jnp.float32), row_block, axis=0), col_block, axis=1)


def fill_rows(target, pieces, half):
    steps, rows = pieces[0].shape[0], pieces[0].shape[1]
    for turn, piece in enumerate(pieces):
        source = jnp.where(half == 0, turn, turn ^ 2)
        target[:, pl.ds(pl.multiple_of(source * rows, rows), rows), :] = piece[...]


def filter_chunk(where, k0, k1, k2, k3, seen, trans_t, dyn_t, packed, maps, shifts, gains):
    width = trans_t.shape[0]
    steps = k0.shape[0]
    fill_rows(gains, (k0, k1, k2, k3), where[0])
    dyn_parts = halves(dyn_t[...])
    running = None
    for step in range(steps):
        gain = halves(gains[step])
        nt = ((1,), (1,))
        seen_rows = rows_of(seen[step : step + 1, :])
        shift = product(halves(seen_rows), gain, nt)
        turned = trans_t[...] - product(dyn_parts, gain, nt)
        if running is None:
            running = (turned, shift)
        else:
            turned = halves(turned)
            running = tuple(product(halves(part), turned, ((1,), (0,))) for part in running)
            running = (running[0], running[1] + shift)
        maps[step] = running[0]
        shifts[step : step + 1, :] = running[1][0:1]
    packed[:width] = running[0]
    packed[width:] = running[1]


def filter_join(where, own, other, before, initial, total, front, state):
    width = own.shape[1]
    late = where[0]

    def follow(early, latter):
        latter_map = halves(latter[:width])
        total_map = product(halves(early[:width]), latter_map, ((1,), (0,)))
        total_shift = product(halves(early[width:]), latter_map, ((1,), (0,))) + latter[width:]
        return total_map, total_shift

    @pl.when(late == 0)
    def _():
        total[:width], total[width:] = follow(own, other)
        front[...] = before[...]

    @pl.when(late != 0)
    def _():
        total[:width], total[width:] = follow(other, own)
        front[:width], front[width:] = follow(other, before)

    state[...] = mm(rows_of(initial[...]), total[:width]) + total[width:]


def filter_last(where, state, initial, before, maps, shifts, means):
    width = before.shape[1]
    steps = maps.shape[0]
    started = jnp.where(where[0] == 0, rows_of(initial[...]), state[...])
    incoming = halves(mm(started, before[:width]) + before[width:])
    for step in range(steps):
        moved = product(incoming, halves(maps[step]), ((1,), (0,)))
        means[step : step + 1, :] = moved[0:1] + shifts[step : step + 1, :]


def smooth_chunk(where, g0, g1, g2, g3, f0, f1, f2, f3, means, trans, noise, packed, maps, covs, offsets, gains, filt, pred):
    width = trans.shape[0]
    steps = g0.shape[0]
    fill_rows(gains, (g0, g1, g2, g3), where[0])
    fill_rows(filt, (f0, f1, f2, f3), where[0])

    @pl.when(where[1] != 0)
    def _():
        gains[steps - 1] = jnp.zeros((width, width), jnp.float32)

    trans_parts = halves(trans[...])
    row_no = lax.broadcasted_iota(jnp.int32, (width, width), 0)
    col_no = lax.broadcasted_iota(jnp.int32, (width, width), 1)
    noise_mat = jnp.where(row_no == col_no, noise[...], 0.0)
    for step in range(steps):
        moved = halves(product(trans_parts, halves(filt[step]), ((1,), (0,))))
        pred[step] = product(moved, trans_parts, ((1,), (1,))) + noise_mat
    cov, mean, chain = None, None, None
    for step in reversed(range(steps)):
        gain = halves(gains[step])
        own_mean = rows_of(means[step : step + 1, :])
        moved_mean = product(halves(own_mean), trans_parts, ((1,), (1,)))
        if cov is None:
            gap, mean_gap, chain = -pred[step], -moved_mean, gains[step]
        else:
            gap, mean_gap = cov - pred[step], mean - moved_mean
            chain = product(gain, halves(chain), ((1,), (0,)))
        gap = halves(product(gain, halves(gap), ((1,), (0,))))
        cov = filt[step] + product(gap, gain, ((1,), (1,)))
        mean = own_mean + product(halves(mean_gap), gain, ((1,), (1,)))
        maps[step] = chain
        covs[step] = cov
        offsets[step : step + 1, :] = mean[0:1]
    packed[:width] = chain
    packed[width : 2 * width] = cov
    packed[2 * width :] = mean


def carry(gain, early_cov, early_mean, cov, mean):
    moved = halves(product(gain, halves(cov), ((1,), (0,))))
    return (
        early_cov + product(moved, gain, ((1,), (1,))),
        early_mean + product(halves(mean), gain, ((1,), (1,))),
    )


def smooth_join(where, own, other, after, total, behind):
    width = own.shape[1]
    late = where[0]

    def follow(early, latter, target):
        gain = halves(early[:width])
        target[:width] = product(gain, halves(latter[:width]), ((1,), (0,)))
        target[width : 2 * width], target[2 * width :] = carry(
            gain,
            early[width : 2 * width],
            early[2 * width :],
            latter[width : 2 * width],
            latter[2 * width :],
        )

    @pl.when(late == 0)
    def _():
        follow(own, other, total)
        follow(after, other, behind)

    @pl.when(late != 0)
    def _():
        follow(other, own, total)
        behind[...] = after[...]


def smooth_last(where, other, after, maps, covs, offsets, p0, p1, p2, p3, start):
    width = after.shape[1]
    steps = maps.shape[0]
    rows = width // 4
    half = where[1]

    @pl.when(where[0] == 0)
    def _():
        start[:width], start[width:] = carry(
            halves(after[:width]),
            after[width : 2 * width],
            after[2 * width :],
            other[:width],
            other[width:],
        )

    @pl.when(where[0] != 0)
    def _():
        start[...] = after[width:]

    begun = halves(start[:width])
    begun_mean = halves(start[width:])
    flip = half != 0
    pieces = (p0, p1, p2, p3)
    mean_rows = []
    for step in range(steps):
        gain = halves(maps[step])
        moved = halves(product(gain, begun, ((1,), (0,))))
        cov = covs[step] + product(moved, gain, ((1,), (1,)))
        mean = product(begun_mean, gain, ((1,), (1,)))
        mean_rows.append(mean[0:1] + offsets[step : step + 1, :])
        for turn, piece in enumerate(pieces):
            block = jnp.where(
                flip,
                cov[rows * (turn ^ 2) : rows * (turn ^ 2) + rows],
                cov[rows * turn : rows * turn + rows],
            )
            piece[step * rows : step * rows + rows] = block
    all_means = jnp.concatenate(mean_rows, axis=0)
    for piece in pieces:
        piece[steps * rows :] = all_means


def call(body, outs, scratch=()):
    def run(where, *operands):
        return pl.pallas_call(
            body,
            out_shape=[jax.ShapeDtypeStruct(shape, jnp.float32) for shape in outs],
            in_specs=[pl.BlockSpec(memory_space=pltpu.SMEM)]
            + [pl.BlockSpec(memory_space=pltpu.VMEM)] * len(operands),
            out_specs=[pl.BlockSpec(memory_space=pltpu.VMEM)] * len(outs),
            scratch_shapes=[pltpu.VMEM(shape, jnp.float32) for shape in scratch],
            compiler_params=pltpu.CompilerParams(vmem_limit_bytes=48 * 1024 * 1024),
        )(jnp.stack([jnp.int32(w) for w in where]), *operands)

    return run


def per_device(
    dynamics,
    dynamics_mask,
    obs_op,
    obs_mask,
    process_noise,
    initial_expectation,
    filter_gains,
    observations,
    smooth_gains,
    filt_cov,
):
    width = dynamics.shape[0]
    obs_width = obs_op.shape[0]
    step_count, row_count = filter_gains.shape[:2]
    steps = step_count // 2
    tm, blk = lax.axis_index("tm"), lax.axis_index("blk")
    tm_count, blk_count = lax.axis_size("tm"), lax.axis_size("blk")
    lines = tm_count // 2
    half = tm % 2
    worker = jnp.logical_or(blk == 1, blk == 2)
    upper = jnp.int32(blk == 2)

    def place(t, z):
        return t * blk_count + z

    def to_workers(array, turn):
        route = [
            (place(2 * line + core, turn ^ (2 * part)), place(2 * line + part, 1 + core))
            for line in range(lines)
            for core in range(2)
            for part in range(2)
        ]
        start = jnp.where(blk == turn, 0, steps)
        return lax.ppermute(lax.dynamic_slice_in_dim(array, start, steps, 0), BOTH, route)

    def from_workers(array, turn):
        route = [
            (place(2 * line + part, 1 + core), place(2 * line + core, turn ^ (2 * part)))
            for line in range(lines)
            for core in range(2)
            for part in range(2)
        ]
        return lax.ppermute(array, BOTH, route)

    levels = [(lambda t, z: (t ^ 1, z), half), (lambda t, z: (t, 3 - z), upper)]
    distance = 2
    while distance < tm_count:
        levels.append((functools.partial(lambda d, t, z: (t ^ d, z), distance), (tm // distance) % 2))
        distance *= 2

    def swap(array, level):
        route = [
            (place(t, z), place(*levels[level][0](t, z))) for t in range(tm_count) for z in (1, 2)
        ]
        return lax.ppermute(array, BOTH, route)

    seen_other = lax.ppermute(observations, "tm", [(t, t ^ 1) for t in range(tm_count)])
    gain_parts = [to_workers(filter_gains, turn) for turn in range(4)]
    smooth_parts = [to_workers(smooth_gains, turn) for turn in range(4)]
    cov_parts = [to_workers(filt_cov, turn) for turn in range(4)]
    seen = jnp.where(half == upper, observations, seen_other)
    seen = lax.dynamic_slice_in_dim(seen, half * steps, steps, 0)

    trans_map = dynamics * expand_mask(dynamics_mask, width, width)
    obs_map = obs_op * expand_mask(obs_mask, obs_width, width)
    obs_dyn = jnp.matmul(obs_map, trans_map, precision=highest)
    initial = initial_expectation[None, :]
    noise = process_noise[None, :]

    packed_filter = (width + PAD, width)
    packed_smooth = (2 * width + PAD, width)
    stack = (steps, width, width)
    short = (steps, width)

    total, maps, shifts = call(filter_chunk, [packed_filter, stack, short], [stack])(
        [half], *gain_parts, seen, trans_map.T, obs_dyn.T
    )
    ident = jnp.eye(width, dtype=jnp.float32)
    front = jnp.concatenate([ident, jnp.zeros((PAD, width), jnp.float32)], axis=0)
    for level in range(len(levels) - 1):
        total, front, state = call(filter_join, [packed_filter, packed_filter, (PAD, width)])(
            [levels[level][1]], total, swap(total, level), front, initial
        )
    (means,) = call(filter_last, [short])(
        [levels[-1][1]], swap(state, len(levels) - 1), initial, front, maps, shifts
    )

    final = jnp.logical_and(tm // 2 == lines - 1, jnp.logical_and(half == 1, blk == 2))
    total, maps, covs, offsets = call(smooth_chunk, [packed_smooth, stack, stack, short], [stack] * 3)(
        [half, final], *smooth_parts, *cov_parts, means, trans_map, noise
    )
    behind = jnp.concatenate([ident, jnp.zeros((width + PAD, width), jnp.float32)], axis=0)
    for level in range(len(levels) - 1):
        total, behind = call(smooth_join, [packed_smooth, packed_smooth])(
            [levels[level][1]], total, swap(total, level), behind
        )
    piece = (steps * row_count + steps, width)
    pieces = call(smooth_last, [piece] * 4, [(width + PAD, width)])(
        [levels[-1][1], half], swap(total[width:], len(levels) - 1), behind, maps, covs, offsets
    )
    arrived = [from_workers(pieces[turn], turn) for turn in range(4)]

    def pick(offset):
        chosen = arrived[0]
        for turn in range(1, 4):
            chosen = jnp.where(blk ^ offset == turn, arrived[turn], chosen)
        return chosen

    chosen = [pick(0), pick(2)]
    cov_out = jnp.concatenate(
        [part[: steps * row_count].reshape(steps, row_count, width) for part in chosen], axis=0
    )
    mean_out = jnp.concatenate([part[steps * row_count :] for part in chosen], axis=0)
    mean_out = lax.dynamic_slice_in_dim(mean_out, blk * row_count, row_count, 1)
    return mean_out, cov_out


def solution(mesh):
    return jax.shard_map(
        per_device,
        mesh=mesh,
        in_specs=(
            P(),
            P(),
            P(),
            P(),
            P(),
            P(),
            P("tm", "blk", None),
            P("tm", None),
            P("tm", "blk", None),
            P("tm", "blk", None),
        ),
        out_specs=(P("tm", "blk"), P("tm", "blk", None)),
        check_vma=False,
    )
```

```python
import functools
import math

import jax
import jax.numpy as jnp
from jax import lax
from jax.experimental import pallas as pl
from jax.experimental.pallas import tpu as pltpu
from jax.sharding import PartitionSpec as P

highest = lax.Precision.HIGHEST
BOTH = ("tm", "blk")
PAD = 16
SPARE = 6 * 1024 * 1024


def halves(x):
    top = x.astype(jnp.bfloat16)
    return top, (x - top.astype(jnp.float32)).astype(jnp.bfloat16)


def product(left, right, dims):
    def one(a, b):
        return lax.dot_general(a, b, (dims, ((), ())), preferred_element_type=jnp.float32)

    rows = left[0].shape[0]
    both = one(jnp.concatenate(left, axis=0), right[0])
    return both[:rows] + (both[rows:] + one(left[0], right[1]))


def mm(left, right):
    return product(halves(left), halves(right), ((1,), (0,)))


def mm_nt(left, right):
    return product(halves(left), halves(right), ((1,), (1,)))


def under(above, below):
    return tuple(jnp.concatenate([a, b], axis=0) for a, b in zip(above, below))


def rows_of(vec):
    return jnp.broadcast_to(vec, (PAD, vec.shape[-1]))


def expand_mask(mask, row_total, col_total):
    row_block = row_total // mask.shape[0]
    col_block = col_total // mask.shape[1]
    return jnp.repeat(jnp.repeat(mask.astype(jnp.float32), row_block, axis=0), col_block, axis=1)


def fill_rows(target, pieces, half):
    rows = pieces[0].shape[1]
    for turn, piece in enumerate(pieces):
        source = jnp.where(half == 0, turn, turn ^ 2)
        target[:, pl.ds(pl.multiple_of(source * rows, rows), rows), :] = piece[...]


def filter_chunk(where, k0, k1, k2, k3, seen, trans_t, dyn_t, packed, maps, shifts, gains):
    width = trans_t.shape[0]
    steps = k0.shape[0]
    fill_rows(gains, (k0, k1, k2, k3), where[0])
    dyn_parts = halves(dyn_t[...])
    running = [None, None]
    for step in range(steps // 2):
        for part in range(2):
            spot = step + part * (steps // 2)
            gain = halves(gains[spot])
            seen_rows = halves(rows_of(seen[spot : spot + 1, :]))
            turned = product(under(dyn_parts, seen_rows), gain, ((1,), (1,)))
            shift = turned[width:]
            turned = trans_t[...] - turned[:width]
            if step == 0:
                running[part] = (turned, shift)
            else:
                running[part] = filter_follow(*running[part], turned, shift)
            maps[spot] = running[part][0]
            shifts[spot : spot + 1, :] = running[part][1][0:1]
    packed[:width], packed[width:] = filter_follow(*running[0], *running[1])


def filter_follow(early_map, early_shift, late_map, late_shift):
    width = late_map.shape[0]
    moved = product(
        under(halves(early_map), halves(early_shift)), halves(late_map), ((1,), (0,))
    )
    return moved[:width], moved[width:] + late_shift


def filter_join(where, own, other, initial, *rest):
    total, state = rest[-2:]
    width = own.shape[1]

    def follow(early, latter):
        total[:width], total[width:] = filter_follow(
            early[:width], early[width:], latter[:width], latter[width:]
        )

    @pl.when(where[0] == 0)
    def _():
        follow(own, other)

    @pl.when(where[0] != 0)
    def _():
        follow(other, own)

    state[...] = mm(rows_of(initial[...]), total[:width]) + total[width:]


def filter_front(where, other, before, front):
    width = before.shape[1]

    @pl.when(where[0] == 0)
    def _():
        front[...] = before[...]

    @pl.when(where[0] != 0)
    def _():
        front[:width], front[width:] = filter_follow(
            other[:width], other[width:], before[:width], before[width:]
        )


def filter_reach(where, state, initial, before, own, reached, onward):
    width = before.shape[1]
    started = jnp.where(where[0] == 0, rows_of(initial[...]), state[...])
    reached[...] = mm(started, before[:width]) + before[width:]
    onward[...] = mm(reached[...], own[:width]) + own[width:]


def filter_last(where, reached, onward, maps, shifts, means):
    steps = maps.shape[0]
    middle = steps // 2
    incoming = jnp.where(where[0] == 0, reached[...], onward[...])
    between = mm(incoming, maps[middle - 1]) + shifts[middle - 1 : middle, :]
    starts = (halves(incoming), halves(between))
    for step in range(steps):
        moved = product(starts[step // middle], halves(maps[step]), ((1,), (0,)))
        means[step : step + 1, :] = moved[0:1] + shifts[step : step + 1, :]


def smooth_chunk(
    where, g0, g1, g2, g3, f0, f1, f2, f3, means, trans, noise, packed, maps, covs, offsets, gains, filt, pred
):
    width = trans.shape[0]
    steps = g0.shape[0]
    middle = steps // 2
    fill_rows(gains, (g0, g1, g2, g3), where[0])
    fill_rows(filt, (f0, f1, f2, f3), where[0])
    gains[steps - 1] = jnp.where(where[1] != 0, 0.0, gains[steps - 1])
    trans_parts = halves(trans[...])
    row_no = lax.broadcasted_iota(jnp.int32, (width, width), 0)
    col_no = lax.broadcasted_iota(jnp.int32, (width, width), 1)
    noise_mat = jnp.where(row_no == col_no, noise[...], 0.0)
    moved_means = mm_nt(jnp.concatenate([means[...]] * (PAD // steps), axis=0), trans[...])
    for step in range(steps):
        moved = halves(product(trans_parts, halves(filt[step]), ((1,), (0,))))
        pred[step] = product(moved, trans_parts, ((1,), (1,))) + noise_mat
    state = [None, None]
    for step in reversed(range(middle)):
        for part in range(2):
            spot = step + part * middle
            gain = halves(gains[spot])
            own_mean = rows_of(means[spot : spot + 1, :])
            moved_mean = rows_of(moved_means[spot : spot + 1, :])
            if state[part] is None:
                gap, mean_gap, chain = -pred[spot], -moved_mean, gains[spot]
            else:
                cov, mean, chain = state[part]
                gap, mean_gap = cov - pred[spot], mean - moved_mean
                chain = product(gain, halves(chain), ((1,), (0,)))
            gap = halves(product(gain, halves(gap), ((1,), (0,))))
            moved = product(under(gap, halves(mean_gap)), gain, ((1,), (1,)))
            cov = filt[spot] + moved[:width]
            mean = own_mean + moved[width:]
            state[part] = (cov, mean, chain)
            maps[spot] = chain
            covs[spot] = cov
            offsets[spot : spot + 1, :] = mean[0:1]
    (early_cov, early_mean, early_chain), (cov, mean, chain) = state
    gain = halves(early_chain)
    packed[:width] = product(gain, halves(chain), ((1,), (0,)))
    packed[width : 2 * width], packed[2 * width :] = carry_parts(gain, early_cov, early_mean, cov, mean)


def carry_parts(gain, early_cov, early_mean, cov, mean):
    width = cov.shape[0]
    moved = halves(product(gain, halves(cov), ((1,), (0,))))
    moved = product(under(moved, halves(mean)), gain, ((1,), (1,)))
    return early_cov + moved[:width], early_mean + moved[width:]


def carry(gain, early, latter):
    width = early.shape[1]
    moved = halves(product(gain, halves(latter[:width]), ((1,), (0,))))
    return early + product(under(moved, halves(latter[width:])), gain, ((1,), (1,)))


def smooth_follow(early, latter, target):
    width = early.shape[1]
    gain = halves(early[:width])
    target[:width] = product(gain, halves(latter[:width]), ((1,), (0,)))
    target[width:] = carry(gain, early[width:], latter[width:])


def smooth_join(where, own, other, total):
    @pl.when(where[0] == 0)
    def _():
        smooth_follow(own, other, total)

    @pl.when(where[0] != 0)
    def _():
        smooth_follow(other, own, total)


def smooth_behind(where, other, after, behind):
    @pl.when(where[0] == 0)
    def _():
        smooth_follow(after, other, behind)

    @pl.when(where[0] != 0)
    def _():
        behind[...] = after[...]


def smooth_reach(where, other, after, reached):
    width = after.shape[1]

    @pl.when(where[0] == 0)
    def _():
        reached[...] = carry(halves(after[:width]), after[width:], other[...])

    @pl.when(where[0] != 0)
    def _():
        reached[...] = after[width:]


def smooth_last(where, own, other, next_total, maps, covs, offsets, p0, p1, p2, p3, start):
    width = maps.shape[1]
    steps = maps.shape[0]
    middle = steps // 2
    rows = width // 4
    half = where[0]

    @pl.when(half == 0)
    def _():
        start[...] = carry(halves(next_total[:width]), next_total[width:], own[...])

    @pl.when(half != 0)
    def _():
        start[...] = other[...]

    late = (start[:width], start[width:])
    early = carry_parts(
        halves(maps[middle]), covs[middle], rows_of(offsets[middle : middle + 1, :]), *late
    )
    starts = [(halves(cov), halves(mean)) for cov, mean in (early, late)]
    pieces = (p0, p1, p2, p3)
    mean_rows = [None] * steps
    for step in reversed(range(steps)):
        gain = halves(maps[step])
        begun, begun_mean = starts[step // middle]
        moved = halves(product(gain, begun, ((1,), (0,))))
        moved = product(under(moved, begun_mean), gain, ((1,), (1,)))
        cov = covs[step] + moved[:width]
        mean_rows[step] = moved[width : width + 1] + offsets[step : step + 1, :]
        for turn, piece in enumerate(pieces):
            swapped = turn ^ 2
            piece[step * rows : step * rows + rows] = jnp.where(
                half == 0,
                cov[rows * turn : rows * turn + rows],
                cov[rows * swapped : rows * swapped + rows],
            )
    all_means = jnp.concatenate(mean_rows, axis=0)
    for piece in pieces:
        piece[steps * rows :] = all_means


def share_halves(where, whole, *rest):
    first, second, sems = rest[-3:]
    steps = first.shape[0]
    flip = where[0]
    copies = [
        pltpu.make_async_copy(whole.at[pl.ds(flip * steps, steps)], first, sems.at[0]),
        pltpu.make_async_copy(whole.at[pl.ds((1 - flip) * steps, steps)], second, sems.at[1]),
    ]
    for copy in copies:
        copy.start()
    for copy in copies:
        copy.wait()


def place_halves(where, a0, a1, a2, a3, mean, cov, seen, sems):
    blk = where[0]
    rows = cov.shape[0] // 2
    short = mean.shape[0] // 2
    wide = mean.shape[1]
    parts = (a0, a1, a2, a3)
    for turn in range(4):

        @pl.when(blk == turn)
        def _(turn=turn):
            copies = []
            for part in range(2):
                source = parts[turn ^ (2 * part)]
                copies.append(
                    pltpu.make_async_copy(
                        source.at[pl.ds(rows, short)], seen.at[pl.ds(part * short, short)], sems.at[part]
                    )
                )
                copies.append(
                    pltpu.make_async_copy(
                        source.at[pl.ds(0, rows)], cov.at[pl.ds(part * rows, rows)], sems.at[2 + part]
                    )
                )
            for copy in copies:
                copy.start()
            for copy in copies:
                copy.wait()
            mean[...] = seen[:, wide * turn : wide * turn + wide]


def call(body, outs, scratch=(), sems=(), far=(), far_outs=()):
    def space(flag):
        return pl.BlockSpec(memory_space=pl.ANY if flag else pltpu.VMEM)

    def run(where, *operands):
        count = len(operands)
        held = [outs[n] for n in range(len(outs)) if n not in far_outs] + list(scratch)
        held += [op.shape for n, op in enumerate(operands) if n not in far and n - count not in far]
        grant = 4 * sum(math.prod(shape) for shape in held) + SPARE
        return pl.pallas_call(
            body,
            out_shape=[jax.ShapeDtypeStruct(shape, jnp.float32) for shape in outs],
            in_specs=[pl.BlockSpec(memory_space=pltpu.SMEM)]
            + [space(n in far or n - count in far) for n in range(count)],
            out_specs=[space(n in far_outs) for n in range(len(outs))],
            scratch_shapes=[pltpu.VMEM(shape, jnp.float32) for shape in scratch]
            + ([pltpu.SemaphoreType.DMA(sems)] if sems else []),
            compiler_params=pltpu.CompilerParams(vmem_limit_bytes=grant),
        )(jnp.stack([jnp.int32(w) for w in where]), *operands)

    return run


def per_device(
    dynamics,
    dynamics_mask,
    obs_op,
    obs_mask,
    process_noise,
    initial_expectation,
    filter_gains,
    observations,
    smooth_gains,
    filt_cov,
):
    width = dynamics.shape[0]
    obs_width = obs_op.shape[0]
    step_count, row_count = filter_gains.shape[:2]
    steps = step_count // 2
    tm, blk = lax.axis_index("tm"), lax.axis_index("blk")
    tm_count, blk_count = lax.axis_size("tm"), lax.axis_size("blk")
    lines = tm_count // 2
    half = tm % 2
    worker = jnp.logical_or(blk == 1, blk == 2)
    upper = jnp.int32(blk == 2)

    def place(t, z):
        return t * blk_count + z

    def to_workers(array, *after):
        shape = (steps,) + array.shape[1:]
        shares = call(
            share_halves, [shape] * 2, sems=(2,), far=range(1 + len(after)), far_outs=range(2)
        )([jnp.int32(blk >= 2)], array, *after)
        arrived = []
        for turn in range(4):
            route = [
                (place(2 * line + core, turn ^ (2 * part)), place(2 * line + part, 1 + core))
                for line in range(lines)
                for core in range(2)
                for part in range(2)
            ]
            arrived.append(lax.ppermute(shares[turn // 2], BOTH, route))
        return arrived

    def from_workers(array, turn):
        route = [
            (place(2 * line + part, 1 + core), place(2 * line + core, turn ^ (2 * part)))
            for line in range(lines)
            for core in range(2)
            for part in range(2)
        ]
        return lax.ppermute(array, BOTH, route)

    levels = [(lambda t, z: (t ^ 1, z), half), (lambda t, z: (t, 3 - z), upper)]
    distance = 2
    while distance < tm_count:
        levels.append((functools.partial(lambda d, t, z: (t ^ d, z), distance), (tm // distance) % 2))
        distance *= 2

    def swap(array, level, cores=(0, 1)):
        route = [
            (place(t, z), place(*levels[level][0](t, z)))
            for t in range(tm_count)
            for z in (1, 2)
            if t % 2 in cores
        ]
        return lax.ppermute(array, BOTH, route)

    seen_other = lax.ppermute(observations, "tm", [(t, t ^ 1) for t in range(tm_count)])
    gain_parts = to_workers(filter_gains)
    smooth_parts = to_workers(smooth_gains)
    seen = jnp.where(half == upper, observations, seen_other)
    seen = lax.dynamic_slice_in_dim(seen, half * steps, steps, 0)

    trans_map = dynamics * expand_mask(dynamics_mask, width, width)
    obs_map = obs_op * expand_mask(obs_mask, obs_width, width)
    obs_dyn = jnp.matmul(obs_map, trans_map, precision=highest)
    initial = initial_expectation[None, :]
    noise = process_noise[None, :]

    packed_filter = (width + PAD, width)
    packed_smooth = (2 * width + PAD, width)
    stack = (steps, width, width)
    short = (steps, width)

    chunk, maps, shifts = call(filter_chunk, [packed_filter, stack, short], [stack])(
        [half], *gain_parts, seen, trans_map.T, obs_dyn.T
    )
    ident = jnp.eye(width, dtype=jnp.float32)
    front = jnp.concatenate([ident, jnp.zeros((PAD, width), jnp.float32)], axis=0)
    total, arrived = chunk, swap(chunk, 0, (1,))
    for level in range(len(levels) - 1):
        late = levels[level][1] if level else 0
        after = (smooth_parts[:2], smooth_parts[2:])[level] if level < 2 else []
        total, state = call(
            filter_join, [packed_filter, (PAD, width)], far=range(-len(after), 0)
        )([late], total, arrived, initial, *after)
        if level:
            (front,) = call(filter_front, [packed_filter])([late], arrived, front)
        else:
            cov_parts = to_workers(filt_cov, state)
        if level < len(levels) - 2:
            arrived = swap(total, level + 1, (0,))
    reached, onward = call(filter_reach, [(PAD, width)] * 2)(
        [levels[-1][1]], swap(state, len(levels) - 1, (0,)), initial, front, chunk
    )
    (means,) = call(filter_last, [short])(
        [half], reached, swap(onward, 0, (0,)), maps, shifts
    )

    final = jnp.logical_and(tm // 2 == lines - 1, jnp.logical_and(half == 1, blk == 2))
    total, maps, covs, offsets = call(
        smooth_chunk, [packed_smooth, stack, stack, short], [stack] * 3
    )([half, final], *smooth_parts, *cov_parts, means, trans_map, noise)
    behind = jnp.concatenate([ident, jnp.zeros((width + PAD, width), jnp.float32)], axis=0)
    next_total = swap(total, 0, (1,))
    (total,) = call(smooth_join, [packed_smooth])([0], total, next_total)
    for level in range(1, len(levels) - 1):
        arrived = swap(total, level, (0,))
        late = levels[level][1]
        (total,) = call(smooth_join, [packed_smooth])([late], total, arrived)
        (behind,) = call(smooth_behind, [packed_smooth])([late], arrived, behind)
    arrived = swap(total[width:], len(levels) - 1, (0,))
    (reached,) = call(smooth_reach, [packed_filter])([levels[-1][1]], arrived, behind)
    piece = (steps * row_count + steps, width)
    pieces = call(smooth_last, [piece] * 4, [packed_filter])(
        [half], reached, swap(reached, 0, (0,)), next_total, maps, covs, offsets
    )
    arrived = [from_workers(pieces[turn], turn) for turn in range(4)]

    mean_out, cov_out = call(
        place_halves,
        [(step_count, row_count), (step_count * row_count, width)],
        [(step_count, width)],
        sems=(4,),
        far=range(4),
        far_outs=[1],
    )([blk], *arrived)
    return mean_out, cov_out.reshape(step_count, row_count, width)


def solution(mesh):
    return jax.shard_map(
        per_device,
        mesh=mesh,
        in_specs=(
            P(),
            P(),
            P(),
            P(),
            P(),
            P(),
            P("tm", "blk", None),
            P("tm", None),
            P("tm", "blk", None),
            P("tm", "blk", None),
        ),
        out_specs=(P("tm", "blk"), P("tm", "blk", None)),
        check_vma=False,
    )
```

```python
import functools
import math

import jax
import jax.numpy as jnp
from jax import lax
from jax.experimental import pallas as pl
from jax.experimental.pallas import tpu as pltpu
from jax.sharding import PartitionSpec as P

highest = lax.Precision.HIGHEST
BOTH = ("tm", "blk")
PAD = 16
CUTS = 4
SPARE = 4 * 1024 * 1024


def halves(x):
    top = x.astype(jnp.bfloat16)
    return top, (x - top.astype(jnp.float32)).astype(jnp.bfloat16)


def product(left, right, dims):
    def one(a, b):
        return lax.dot_general(a, b, (dims, ((), ())), preferred_element_type=jnp.float32)

    rows = left[0].shape[0]
    both = one(jnp.concatenate(left, axis=0), right[0])
    return both[:rows] + (both[rows:] + one(left[0], right[1]))


def mm(left, right):
    return product(halves(left), halves(right), ((1,), (0,)))


def mm_nt(left, right):
    return product(halves(left), halves(right), ((1,), (1,)))


def under(above, below):
    return tuple(jnp.concatenate([a, b], axis=0) for a, b in zip(above, below))


def rows_of(vec):
    return jnp.broadcast_to(vec, (PAD, vec.shape[-1]))


def expand_mask(mask, row_total, col_total):
    row_block = row_total // mask.shape[0]
    col_block = col_total // mask.shape[1]
    return jnp.repeat(jnp.repeat(mask.astype(jnp.float32), row_block, axis=0), col_block, axis=1)


def whole(pieces, step, half, latter=0):
    parts = [piece[step + latter * (piece.shape[0] - pieces[0].shape[0])] for piece in pieces]
    straight = jnp.concatenate(parts, axis=0)
    return jnp.where(half == 0, straight, jnp.concatenate(parts[2:] + parts[:2], axis=0))


def filter_chunk(where, k0, k1, k2, k3, seen, trans_t, dyn_t, *rest):
    packed, maps, shifts = rest[-3:]
    width = trans_t.shape[0]
    steps = k0.shape[0]
    dyn_parts = halves(dyn_t[...])
    running = [None, None]
    for step in range(steps // 2):
        for part in range(2):
            spot = step + part * (steps // 2)
            gain = halves(whole((k0, k1, k2, k3), spot, where[0]))
            seen_rows = halves(rows_of(seen[spot : spot + 1, :]))
            turned = product(under(dyn_parts, seen_rows), gain, ((1,), (1,)))
            shift = turned[width:]
            turned = trans_t[...] - turned[:width]
            if step == 0:
                running[part] = (turned, shift)
            else:
                running[part] = filter_follow(*running[part], turned, shift)
            maps[spot] = running[part][0]
            shifts[spot : spot + 1, :] = running[part][1][0:1]
    packed[:width], packed[width:] = filter_follow(*running[0], *running[1])


def filter_follow(early_map, early_shift, late_map, late_shift):
    width = late_map.shape[0]
    moved = product(
        under(halves(early_map), halves(early_shift)), halves(late_map), ((1,), (0,))
    )
    return moved[:width], moved[width:] + late_shift


def filter_join(where, own, other, initial, *rest):
    total, state = rest[-2:]
    width = own.shape[1]

    def follow(early, latter):
        total[:width], total[width:] = filter_follow(
            early[:width], early[width:], latter[:width], latter[width:]
        )

    @pl.when(where[0] == 0)
    def _():
        follow(own, other)

    @pl.when(where[0] != 0)
    def _():
        follow(other, own)

    state[...] = mm(rows_of(initial[...]), total[:width]) + total[width:]


def filter_reach(where, state, initial, own, *rest):
    reached, onward = rest[-2:]
    width = own.shape[1]
    current = jnp.where(where[0] == 0, rows_of(initial[...]), state[...])
    for n, other in enumerate(rest[:-2]):
        moved = mm(current, other[:width]) + other[width:]
        current = jnp.where(where[1 + n] == 0, current, moved)
    reached[...] = current
    onward[...] = mm(current, own[:width]) + own[width:]


def filter_last(where, reached, onward, maps, shifts, means):
    steps = maps.shape[0]
    middle = steps // 2
    incoming = jnp.where(where[0] == 0, reached[...], onward[...])
    between = mm(incoming, maps[middle - 1]) + shifts[middle - 1 : middle, :]
    starts = (halves(incoming), halves(between))
    for step in range(steps):
        moved = product(starts[step // middle], halves(maps[step]), ((1,), (0,)))
        means[step : step + 1, :] = moved[0:1] + shifts[step : step + 1, :]


def predict(where, f0, f1, f2, f3, trans, noise, after, filt, pred):
    width = trans.shape[0]
    steps = f0.shape[0]
    trans_parts = halves(trans[...])
    row_no = lax.broadcasted_iota(jnp.int32, (width, width), 0)
    col_no = lax.broadcasted_iota(jnp.int32, (width, width), 1)
    noise_mat = jnp.where(row_no == col_no, noise[...], 0.0)
    for step in range(steps):
        now = whole((f0, f1, f2, f3), step, where[0])
        filt[step] = now
        moved = halves(product(trans_parts, halves(now), ((1,), (0,))))
        pred[step] = product(moved, trans_parts, ((1,), (1,))) + noise_mat


def smooth_chunk(where, g0, g1, g2, g3, filt, pred, after, packed, maps, covs):
    width = filt.shape[1]
    steps = g0.shape[0]
    middle = steps // 2
    state = [None, None]
    for step in reversed(range(middle)):
        for part in range(2):
            spot = step + part * middle
            gain_now = whole((g0, g1, g2, g3), spot, where[0], 1)
            if spot == steps - 1:
                gain_now = jnp.where(where[1] != 0, 0.0, gain_now)
            gain = halves(gain_now)
            if state[part] is None:
                gap, chain = -pred[spot], gain_now
            else:
                cov, chain = state[part]
                gap = cov - pred[spot]
                chain = product(gain, halves(chain), ((1,), (0,)))
            gap = halves(product(gain, halves(gap), ((1,), (0,))))
            cov = filt[spot] + product(gap, gain, ((1,), (1,)))
            state[part] = (cov, chain)
            maps[spot] = chain
            covs[spot] = cov
    (early_cov, early_chain), (cov, chain) = state
    gain = halves(early_chain)
    packed[:width] = product(gain, halves(chain), ((1,), (0,)))
    moved = halves(product(gain, halves(cov), ((1,), (0,))))
    packed[width:] = early_cov + product(moved, gain, ((1,), (1,)))


def smooth_offsets(where, g0, g1, g2, g3, means, trans, maps, offsets, delta):
    steps = g0.shape[0]
    middle = steps // 2
    moved_means = mm_nt(jnp.concatenate([means[...]] * (PAD // steps), axis=0), trans[...])
    state = [None, None]
    for step in reversed(range(middle)):
        for part in range(2):
            spot = step + part * middle
            gain_now = whole((g0, g1, g2, g3), spot, where[0], 1)
            if spot == steps - 1:
                gain_now = jnp.where(where[1] != 0, 0.0, gain_now)
            gap = -rows_of(moved_means[spot : spot + 1, :])
            if state[part] is not None:
                gap = state[part] + gap
            state[part] = rows_of(means[spot : spot + 1, :]) + mm_nt(gap, gain_now)
            offsets[spot : spot + 1, :] = state[part][0:1]
    delta[...] = state[0] + mm_nt(state[1], maps[0])


def smooth_join_cov(where, own, other, total):
    width = own.shape[1]
    gain = halves(own[:width])
    total[:width] = product(gain, halves(other[:width]), ((1,), (0,)))
    moved = halves(product(gain, halves(other[width:]), ((1,), (0,))))
    total[width:] = own[width:] + product(moved, gain, ((1,), (1,)))


def smooth_join_delta(where, own, delta, other, total):
    total[...] = delta[...] + mm_nt(other[...], own[: own.shape[1]])


def carry_parts(gain, early_cov, early_mean, cov, mean):
    width = cov.shape[0]
    moved = halves(product(gain, halves(cov), ((1,), (0,))))
    moved = product(under(moved, halves(mean)), gain, ((1,), (1,)))
    return early_cov + moved[:width], early_mean + moved[width:]


def carry(gain, early, latter):
    width = early.shape[1]
    moved = halves(product(gain, halves(latter[:width]), ((1,), (0,))))
    return early + product(under(moved, halves(latter[width:])), gain, ((1,), (1,)))


def smooth_follow(early, latter, target):
    width = early.shape[1]
    gain = halves(early[:width])
    target[:width] = product(gain, halves(latter[:width]), ((1,), (0,)))
    target[width:] = carry(gain, early[width:], latter[width:])


def smooth_join(where, own, other, total):
    @pl.when(where[0] == 0)
    def _():
        smooth_follow(own, other, total)

    @pl.when(where[0] != 0)
    def _():
        smooth_follow(other, own, total)


def smooth_behind(where, other, after, behind):
    @pl.when(where[0] == 0)
    def _():
        smooth_follow(after, other, behind)

    @pl.when(where[0] != 0)
    def _():
        behind[...] = after[...]


def smooth_reach(where, other, after, reached):
    width = after.shape[1]

    @pl.when(where[0] == 0)
    def _():
        reached[...] = carry(halves(after[:width]), after[width:], other[...])

    @pl.when(where[0] != 0)
    def _():
        reached[...] = after[width:]


def smooth_last(where, own, other, next_total, maps, covs, offsets, p0, p1, p2, p3, start):
    width = maps.shape[1]
    steps = maps.shape[0]
    middle = steps // 2
    rows = width // 4
    half = where[0]

    @pl.when(half == 0)
    def _():
        start[...] = carry(halves(next_total[:width]), next_total[width:], own[...])

    @pl.when(half != 0)
    def _():
        start[...] = other[...]

    late = (start[:width], start[width:])
    early = carry_parts(
        halves(maps[middle]), covs[middle], rows_of(offsets[middle : middle + 1, :]), *late
    )
    starts = [(halves(cov), halves(mean)) for cov, mean in (early, late)]
    pieces = (p0, p1, p2, p3)
    mean_rows = [None] * steps
    for step in reversed(range(steps)):
        gain = halves(maps[step])
        begun, begun_mean = starts[step // middle]
        moved = halves(product(gain, begun, ((1,), (0,))))
        moved = product(under(moved, begun_mean), gain, ((1,), (1,)))
        cov = covs[step] + moved[:width]
        mean_rows[step] = moved[width : width + 1] + offsets[step : step + 1, :]
        for turn, piece in enumerate(pieces):
            swapped = turn ^ 2
            piece[step * rows : step * rows + rows] = jnp.where(
                half == 0,
                cov[rows * turn : rows * turn + rows],
                cov[rows * swapped : rows * swapped + rows],
            )
    all_means = jnp.concatenate(mean_rows, axis=0)
    for piece in pieces:
        piece[steps * rows :] = all_means


def share_half(where, *refs):
    share = refs[-1]
    wholes = refs[:-1]
    steps = wholes[0].shape[0] // 2

    @pl.when(where[0] == 0)
    def _():
        for n in range(share.shape[0] // steps):
            share[n * steps : n * steps + steps] = wholes[n][:steps]

    @pl.when(where[0] != 0)
    def _():
        for n in range(share.shape[0] // steps):
            share[n * steps : n * steps + steps] = wholes[n][steps:]


def place_halves(where, a0, a1, a2, a3, mean, cov, seen, sems):
    blk = where[0]
    rows = cov.shape[0] // 2
    short = mean.shape[0] // 2
    wide = mean.shape[1]
    parts = (a0, a1, a2, a3)
    cut = rows // CUTS
    for turn in range(4):

        @pl.when(blk == turn)
        def _(turn=turn):
            copies = []
            for part in range(2):
                source = parts[turn ^ (2 * part)]
                pairs = [(source.at[pl.ds(rows, short)], seen.at[pl.ds(part * short, short)])]
                for n in range(CUTS):
                    spot = pl.ds(part * rows + n * cut, cut)
                    pairs.append((source.at[pl.ds(n * cut, cut)], cov.at[spot]))
                for n, pair in enumerate(pairs):
                    copies.append(pltpu.make_async_copy(*pair, sems.at[part, n]))
                    copies[-1].start()
            for copy in copies:
                copy.wait()
            mean[...] = seen[:, wide * turn : wide * turn + wide]


def call(body, outs, scratch=(), sems=(), far=(), far_outs=(), alias=(), grant=None):
    def space(flag):
        return pl.BlockSpec(memory_space=pl.ANY if flag else pltpu.VMEM)

    def run(where, *operands):
        count = len(operands)
        held = [outs[n] for n in range(len(outs)) if n not in far_outs and n not in [b for _, b in alias]] + list(scratch)
        held += [op.shape for n, op in enumerate(operands) if n not in far and n - count not in far]
        limit = grant or 4 * sum(math.prod(shape) for shape in held) + SPARE
        return pl.pallas_call(
            body,
            out_shape=[jax.ShapeDtypeStruct(shape, jnp.float32) for shape in outs],
            in_specs=[pl.BlockSpec(memory_space=pltpu.SMEM)]
            + [space(n in far or n - count in far) for n in range(count)],
            out_specs=[space(n in far_outs) for n in range(len(outs))],
            scratch_shapes=[pltpu.VMEM(shape, jnp.float32) for shape in scratch]
            + ([pltpu.SemaphoreType.DMA(sems)] if sems else []),
            input_output_aliases={1 + a: b for a, b in alias},
            compiler_params=pltpu.CompilerParams(vmem_limit_bytes=limit),
        )(jnp.stack([jnp.int32(w) for w in where]), *operands)

    return run


def per_device(
    dynamics,
    dynamics_mask,
    obs_op,
    obs_mask,
    process_noise,
    initial_expectation,
    filter_gains,
    observations,
    smooth_gains,
    filt_cov,
):
    width = dynamics.shape[0]
    obs_width = obs_op.shape[0]
    step_count, row_count = filter_gains.shape[:2]
    steps = step_count // 2
    tm, blk = lax.axis_index("tm"), lax.axis_index("blk")
    tm_count, blk_count = lax.axis_size("tm"), lax.axis_size("blk")
    lines = tm_count // 2
    half = tm % 2
    worker = jnp.logical_or(blk == 1, blk == 2)
    upper = jnp.int32(blk == 2)

    def place(t, z):
        return t * blk_count + z

    def share(arrays, latter):
        flip = jnp.int32((blk >= 2) != latter)
        shape = (steps * len(arrays),) + arrays[0].shape[1:]
        return call(share_half, [shape])([flip], *arrays)[0]

    def to_workers(array, turn):
        pairs = [
            (place(2 * line + core, turn ^ (2 * part)), place(2 * line + part, 1 + core))
            for line in range(lines)
            for core in range(2)
            for part in range(2)
        ]
        return lax.ppermute(array, BOTH, pairs)

    def from_workers(array, turn):
        route = [
            (place(2 * line + part, 1 + core), place(2 * line + core, turn ^ (2 * part)))
            for line in range(lines)
            for core in range(2)
            for part in range(2)
        ]
        return lax.ppermute(array, BOTH, route)

    levels = [(lambda t, z: (t ^ 1, z), half), (lambda t, z: (t, 3 - z), upper)]
    distance = 2
    while distance < tm_count:
        levels.append((functools.partial(lambda d, t, z: (t ^ d, z), distance), (tm // distance) % 2))
        distance *= 2

    def swap(array, level, cores=(0, 1)):
        route = [
            (place(t, z), place(*levels[level][0](t, z)))
            for t in range(tm_count)
            for z in (1, 2)
            if t % 2 in cores
        ]
        return lax.ppermute(array, BOTH, route)

    seen_other = lax.ppermute(observations, "tm", [(t, t ^ 1) for t in range(tm_count)])
    gain_shares = [share([filter_gains], latter) for latter in (False, True)]
    gain_parts = [to_workers(gain_shares[turn // 2], turn) for turn in range(4)]
    cov_shares = [share([filt_cov], latter) for latter in (False, True)]
    cov_parts = [to_workers(cov_shares[turn // 2], turn) for turn in range(4)]
    late_shares = [share([smooth_gains], latter) for latter in (False, True)]
    seen = jnp.where(half == upper, observations, seen_other)
    seen = lax.dynamic_slice_in_dim(seen, half * steps, steps, 0)

    trans_map = dynamics * expand_mask(dynamics_mask, width, width)
    obs_map = obs_op * expand_mask(obs_mask, obs_width, width)
    obs_dyn = jnp.matmul(obs_map, trans_map, precision=highest)
    initial = initial_expectation[None, :]
    noise = process_noise[None, :]

    packed_filter = (width + PAD, width)
    packed_smooth = (2 * width + PAD, width)
    stack = (steps, width, width)
    short = (steps, width)

    chunk, maps, shifts = call(filter_chunk, [packed_filter, stack, short], far=[-2, -1])(
        [half], *gain_parts, seen, trans_map.T, obs_dyn.T, *late_shares
    )
    total, arrived, others = chunk, swap(chunk, 0, (1,)), []
    for level in range(len(levels) - 1):
        after = (cov_parts[:2], cov_parts[2:])[level] if level < 2 else []
        total, state = call(
            filter_join, [packed_filter, (PAD, width)], far=range(-len(after), 0)
        )([levels[level][1] if level else 0], total, arrived, initial, *after)
        if level == 1:
            filt, pred = call(predict, [stack] * 2, far=[-1])(
                [half], *cov_parts, trans_map, noise, state
            )
        if level:
            others.insert(0, (levels[level][1], arrived))
        else:
            *late_shares, total = lax.optimization_barrier((*late_shares, total))
            smooth_parts = [to_workers(late_shares[turn // 2], turn) for turn in range(4)]
        if level < len(levels) - 2:
            arrived = swap(total, level + 1, (0,))
    reached, onward = call(filter_reach, [(PAD, width)] * 2)(
        [levels[-1][1]] + [late for late, _ in others],
        swap(state, len(levels) - 1, (0,)),
        initial,
        chunk,
        *[arrived for _, arrived in others],
    )
    (means,) = call(filter_last, [short])(
        [half], reached, swap(onward, 0, (0,)), maps, shifts
    )

    final = jnp.logical_and(tm // 2 == lines - 1, jnp.logical_and(half == 1, blk == 2))
    plain = (2 * width, width)
    first, maps, covs = call(smooth_chunk, [plain, stack, stack], alias=[(5, 1), (4, 2)], far=[-1])(
        [half, final], *smooth_parts, filt, pred, means
    )
    offsets, delta = call(smooth_offsets, [short, (PAD, width)])(
        [half, final], *smooth_parts, means, trans_map, maps
    )
    next_cov = swap(first, 0, (1,))
    (total,) = call(smooth_join_cov, [plain])([0], first, next_cov)
    next_delta = swap(delta, 0, (1,))
    (delta,) = call(smooth_join_delta, [(PAD, width)])([0], first, delta, next_delta)
    behind = None
    for level in range(1, len(levels) - 1):
        arrived = swap(total, level, (0,))
        if behind is None:
            arrived = jnp.concatenate([arrived, swap(delta, level, (0,))], axis=0)
            total = jnp.concatenate([total, delta], axis=0)
        late = levels[level][1]
        (total,) = call(smooth_join, [packed_smooth])([late], total, arrived)
        if behind is None:
            behind = jnp.where(late == 0, arrived, jnp.eye(*packed_smooth, dtype=jnp.float32))
        else:
            (behind,) = call(smooth_behind, [packed_smooth])([late], arrived, behind)
    next_total = jnp.concatenate([next_cov, next_delta], axis=0)
    arrived = swap(total[width:], len(levels) - 1, (0,))
    (reached,) = call(smooth_reach, [packed_filter])([levels[-1][1]], arrived, behind)
    piece = (steps * row_count + steps, width)
    pieces = call(smooth_last, [piece] * 4, [packed_filter])(
        [half], reached, swap(reached, 0, (0,)), next_total, maps, covs, offsets
    )
    arrived = [from_workers(pieces[turn], turn) for turn in range(4)]

    mean_out, cov_out = call(
        place_halves,
        [(step_count, row_count), (step_count * row_count, width)],
        [(step_count, width)],
        sems=(2, CUTS + 1),
        far=range(4),
        far_outs=[1],
    )([blk], *arrived)
    return mean_out, cov_out.reshape(step_count, row_count, width)


def solution(mesh):
    return jax.shard_map(
        per_device,
        mesh=mesh,
        in_specs=(
            P(),
            P(),
            P(),
            P(),
            P(),
            P(),
            P("tm", "blk", None),
            P("tm", None),
            P("tm", "blk", None),
            P("tm", "blk", None),
        ),
        out_specs=(P("tm", "blk"), P("tm", "blk", None)),
        check_vma=False,
    )
```

```python
import functools
import math

import jax
import jax.numpy as jnp
from jax import lax
from jax.experimental import pallas as pl
from jax.experimental.pallas import tpu as pltpu
from jax.sharding import PartitionSpec as P

highest = lax.Precision.HIGHEST
BOTH = ("tm", "blk")
PAD = 16
CUTS = 4
SPARE = 4 * 1024 * 1024


def halves(x):
    top = x.astype(jnp.bfloat16)
    return top, (x - top.astype(jnp.float32)).astype(jnp.bfloat16)


def product(left, right, dims):
    def one(a, b):
        return lax.dot_general(a, b, (dims, ((), ())), preferred_element_type=jnp.float32)

    rows = left[0].shape[0]
    both = one(jnp.concatenate(left, axis=0), right[0])
    return both[:rows] + (both[rows:] + one(left[0], right[1]))


def mm(left, right):
    return product(halves(left), halves(right), ((1,), (0,)))


def mm_nt(left, right):
    return product(halves(left), halves(right), ((1,), (1,)))


def under(above, below):
    return tuple(jnp.concatenate([a, b], axis=0) for a, b in zip(above, below))


def rows_of(vec):
    return jnp.broadcast_to(vec, (PAD, vec.shape[-1]))


def expand_mask(mask, row_total, col_total):
    row_block = row_total // mask.shape[0]
    col_block = col_total // mask.shape[1]
    return jnp.repeat(jnp.repeat(mask.astype(jnp.float32), row_block, axis=0), col_block, axis=1)


def whole(pieces, step, half, latter=0):
    parts = [piece[step + latter * (piece.shape[0] - pieces[0].shape[0])] for piece in pieces]
    straight = jnp.concatenate(parts, axis=0)
    return jnp.where(half == 0, straight, jnp.concatenate(parts[2:] + parts[:2], axis=0))


def filter_chunk(where, k0, k1, k2, k3, seen, trans_t, dyn_t, *rest):
    packed, maps, shifts = rest[-3:]
    width = trans_t.shape[0]
    steps = k0.shape[0]
    dyn_parts = halves(dyn_t[...])
    running = [None, None]
    for step in range(steps // 2):
        for part in range(2):
            spot = step + part * (steps // 2)
            gain = halves(whole((k0, k1, k2, k3), spot, where[0]))
            seen_rows = halves(rows_of(seen[spot : spot + 1, :]))
            turned = product(under(dyn_parts, seen_rows), gain, ((1,), (1,)))
            shift = turned[width:]
            turned = trans_t[...] - turned[:width]
            if step == 0:
                running[part] = (turned, shift)
            else:
                running[part] = filter_follow(*running[part], turned, shift)
            maps[spot] = running[part][0]
            shifts[spot : spot + 1, :] = running[part][1][0:1]
    packed[:width], packed[width:] = filter_follow(*running[0], *running[1])


def filter_follow(early_map, early_shift, late_map, late_shift):
    width = late_map.shape[0]
    moved = product(
        under(halves(early_map), halves(early_shift)), halves(late_map), ((1,), (0,))
    )
    return moved[:width], moved[width:] + late_shift


def filter_join(where, own, other, initial, *rest):
    total, state = rest[-2:]
    width = own.shape[1]

    def follow(early, latter):
        total[:width], total[width:] = filter_follow(
            early[:width], early[width:], latter[:width], latter[width:]
        )

    @pl.when(where[0] == 0)
    def _():
        follow(own, other)

    @pl.when(where[0] != 0)
    def _():
        follow(other, own)

    state[...] = mm(rows_of(initial[...]), total[:width]) + total[width:]


def filter_reach(where, state, initial, own, *rest):
    reached, onward = rest[-2:]
    width = own.shape[1]
    current = jnp.where(where[0] == 0, rows_of(initial[...]), state[...])
    for n, other in enumerate(rest[:-2]):
        moved = mm(current, other[:width]) + other[width:]
        current = jnp.where(where[1 + n] == 0, current, moved)
    reached[...] = current
    onward[...] = mm(current, own[:width]) + own[width:]


def filter_last(where, reached, onward, maps, shifts, means):
    steps = maps.shape[0]
    middle = steps // 2
    incoming = jnp.where(where[0] == 0, reached[...], onward[...])
    between = mm(incoming, maps[middle - 1]) + shifts[middle - 1 : middle, :]
    starts = (halves(incoming), halves(between))
    for step in range(steps):
        moved = product(starts[step // middle], halves(maps[step]), ((1,), (0,)))
        means[step : step + 1, :] = moved[0:1] + shifts[step : step + 1, :]


def predict(where, f0, f1, f2, f3, trans, noise, after, filt, pred):
    width = trans.shape[0]
    steps = f0.shape[0]
    trans_parts = halves(trans[...])
    row_no = lax.broadcasted_iota(jnp.int32, (width, width), 0)
    col_no = lax.broadcasted_iota(jnp.int32, (width, width), 1)
    noise_mat = jnp.where(row_no == col_no, noise[...], 0.0)
    for step in range(steps):
        now = whole((f0, f1, f2, f3), step, where[0])
        filt[step] = now
        moved = halves(product(trans_parts, halves(now), ((1,), (0,))))
        pred[step] = product(moved, trans_parts, ((1,), (1,))) + noise_mat


def smooth_chunk(where, g0, g1, g2, g3, filt, pred, after, packed, maps, covs):
    width = filt.shape[1]
    steps = g0.shape[0]
    middle = steps // 2
    state = [None, None]
    for step in reversed(range(middle)):
        for part in range(2):
            spot = step + part * middle
            gain_now = whole((g0, g1, g2, g3), spot, where[0], 1)
            if spot == steps - 1:
                gain_now = jnp.where(where[1] != 0, 0.0, gain_now)
            gain = halves(gain_now)
            if state[part] is None:
                gap, chain = -pred[spot], gain_now
            else:
                cov, chain = state[part]
                gap = cov - pred[spot]
                chain = product(gain, halves(chain), ((1,), (0,)))
            gap = halves(product(gain, halves(gap), ((1,), (0,))))
            cov = filt[spot] + product(gap, gain, ((1,), (1,)))
            state[part] = (cov, chain)
            maps[spot] = chain
            covs[spot] = cov
    (early_cov, early_chain), (cov, chain) = state
    gain = halves(early_chain)
    packed[:width] = product(gain, halves(chain), ((1,), (0,)))
    moved = halves(product(gain, halves(cov), ((1,), (0,))))
    packed[width:] = early_cov + product(moved, gain, ((1,), (1,)))


def smooth_offsets(where, g0, g1, g2, g3, means, trans, maps, offsets, delta):
    steps = g0.shape[0]
    middle = steps // 2
    moved_means = mm_nt(jnp.concatenate([means[...]] * (PAD // steps), axis=0), trans[...])
    state = [None, None]
    for step in reversed(range(middle)):
        for part in range(2):
            spot = step + part * middle
            gain_now = whole((g0, g1, g2, g3), spot, where[0], 1)
            if spot == steps - 1:
                gain_now = jnp.where(where[1] != 0, 0.0, gain_now)
            gap = -rows_of(moved_means[spot : spot + 1, :])
            if state[part] is not None:
                gap = state[part] + gap
            state[part] = rows_of(means[spot : spot + 1, :]) + mm_nt(gap, gain_now)
            offsets[spot : spot + 1, :] = state[part][0:1]
    delta[...] = state[0] + mm_nt(state[1], maps[0])


def smooth_join_cov(where, own, other, after, total):
    width = own.shape[1]
    gain = halves(own[:width])
    total[:width] = product(gain, halves(other[:width]), ((1,), (0,)))
    moved = halves(product(gain, halves(other[width:]), ((1,), (0,))))
    total[width:] = own[width:] + product(moved, gain, ((1,), (1,)))


def smooth_join_delta(where, own, delta, other, total):
    total[...] = delta[...] + mm_nt(other[...], own[: own.shape[1]])


def carry_parts(gain, early_cov, early_mean, cov, mean):
    width = cov.shape[0]
    moved = halves(product(gain, halves(cov), ((1,), (0,))))
    moved = product(under(moved, halves(mean)), gain, ((1,), (1,)))
    return early_cov + moved[:width], early_mean + moved[width:]


def carry(gain, early, latter):
    width = early.shape[1]
    moved = halves(product(gain, halves(latter[:width]), ((1,), (0,))))
    return early + product(under(moved, halves(latter[width:])), gain, ((1,), (1,)))


def smooth_follow(early, latter, target):
    width = early.shape[1]
    gain = halves(early[:width])
    target[:width] = product(gain, halves(latter[:width]), ((1,), (0,)))
    target[width:] = carry(gain, early[width:], latter[width:])


def smooth_join(where, own, other, total):
    @pl.when(where[0] == 0)
    def _():
        smooth_follow(own, other, total)

    @pl.when(where[0] != 0)
    def _():
        smooth_follow(other, own, total)


def smooth_behind(where, other, after, behind):
    @pl.when(where[0] == 0)
    def _():
        smooth_follow(after, other, behind)

    @pl.when(where[0] != 0)
    def _():
        behind[...] = after[...]


def smooth_reach(where, other, after, reached):
    width = after.shape[1]

    @pl.when(where[0] == 0)
    def _():
        reached[...] = carry(halves(after[:width]), after[width:], other[...])

    @pl.when(where[0] != 0)
    def _():
        reached[...] = after[width:]


def smooth_last(where, own, other, next_total, maps, covs, offsets, p0, p1, p2, p3, start):
    width = maps.shape[1]
    steps = maps.shape[0]
    middle = steps // 2
    rows = width // 4
    half = where[0]

    @pl.when(half == 0)
    def _():
        start[...] = carry(halves(next_total[:width]), next_total[width:], own[...])

    @pl.when(half != 0)
    def _():
        start[...] = other[...]

    late = (start[:width], start[width:])
    early = carry_parts(
        halves(maps[middle]), covs[middle], rows_of(offsets[middle : middle + 1, :]), *late
    )
    starts = [(halves(cov), halves(mean)) for cov, mean in (early, late)]
    pieces = (p0, p1, p2, p3)
    mean_rows = [None] * steps
    for step in reversed(range(steps)):
        gain = halves(maps[step])
        begun, begun_mean = starts[step // middle]
        moved = halves(product(gain, begun, ((1,), (0,))))
        moved = product(under(moved, begun_mean), gain, ((1,), (1,)))
        cov = covs[step] + moved[:width]
        mean_rows[step] = moved[width : width + 1] + offsets[step : step + 1, :]
        for turn, piece in enumerate(pieces):
            swapped = turn ^ 2
            piece[step * rows : step * rows + rows] = jnp.where(
                half == 0,
                cov[rows * turn : rows * turn + rows],
                cov[rows * swapped : rows * swapped + rows],
            )
    all_means = jnp.concatenate(mean_rows, axis=0)
    for piece in pieces:
        piece[steps * rows :] = all_means


def share_half(where, *refs):
    share = refs[-1]
    wholes = refs[:-1]
    steps = wholes[0].shape[0] // 2

    @pl.when(where[0] == 0)
    def _():
        for n in range(share.shape[0] // steps):
            share[n * steps : n * steps + steps] = wholes[n][:steps]

    @pl.when(where[0] != 0)
    def _():
        for n in range(share.shape[0] // steps):
            share[n * steps : n * steps + steps] = wholes[n][steps:]


def place_halves(where, a0, a1, a2, a3, mean, cov, seen, sems):
    blk = where[0]
    rows = cov.shape[0] // 2
    short = mean.shape[0] // 2
    wide = mean.shape[1]
    parts = (a0, a1, a2, a3)
    cut = rows // CUTS
    for turn in range(4):

        @pl.when(blk == turn)
        def _(turn=turn):
            copies = []
            for part in range(2):
                source = parts[turn ^ (2 * part)]
                pairs = [(source.at[pl.ds(rows, short)], seen.at[pl.ds(part * short, short)])]
                for n in range(CUTS):
                    spot = pl.ds(part * rows + n * cut, cut)
                    pairs.append((source.at[pl.ds(n * cut, cut)], cov.at[spot]))
                for n, pair in enumerate(pairs):
                    copies.append(pltpu.make_async_copy(*pair, sems.at[part, n]))
                    copies[-1].start()
            for copy in copies:
                copy.wait()
            mean[...] = seen[:, wide * turn : wide * turn + wide]


def call(body, outs, scratch=(), sems=(), far=(), far_outs=(), alias=(), grant=None):
    def space(flag):
        return pl.BlockSpec(memory_space=pl.ANY if flag else pltpu.VMEM)

    def run(where, *operands):
        count = len(operands)
        held = [outs[n] for n in range(len(outs)) if n not in far_outs and n not in [b for _, b in alias]] + list(scratch)
        held += [op.shape for n, op in enumerate(operands) if n not in far and n - count not in far]
        limit = grant or 4 * sum(math.prod(shape) for shape in held) + SPARE
        return pl.pallas_call(
            body,
            out_shape=[jax.ShapeDtypeStruct(shape, jnp.float32) for shape in outs],
            in_specs=[pl.BlockSpec(memory_space=pltpu.SMEM)]
            + [space(n in far or n - count in far) for n in range(count)],
            out_specs=[space(n in far_outs) for n in range(len(outs))],
            scratch_shapes=[pltpu.VMEM(shape, jnp.float32) for shape in scratch]
            + ([pltpu.SemaphoreType.DMA(sems)] if sems else []),
            input_output_aliases={1 + a: b for a, b in alias},
            compiler_params=pltpu.CompilerParams(vmem_limit_bytes=limit),
        )(jnp.stack([jnp.int32(w) for w in where]), *operands)

    return run


def per_device(
    dynamics,
    dynamics_mask,
    obs_op,
    obs_mask,
    process_noise,
    initial_expectation,
    filter_gains,
    observations,
    smooth_gains,
    filt_cov,
):
    width = dynamics.shape[0]
    obs_width = obs_op.shape[0]
    step_count, row_count = filter_gains.shape[:2]
    steps = step_count // 2
    tm, blk = lax.axis_index("tm"), lax.axis_index("blk")
    tm_count, blk_count = lax.axis_size("tm"), lax.axis_size("blk")
    lines = tm_count // 2
    half = tm % 2
    worker = jnp.logical_or(blk == 1, blk == 2)
    upper = jnp.int32(blk == 2)

    def place(t, z):
        return t * blk_count + z

    def share(arrays, latter):
        flip = jnp.int32((blk >= 2) != latter)
        shape = (steps * len(arrays),) + arrays[0].shape[1:]
        return call(share_half, [shape])([flip], *arrays)[0]

    def to_workers(array, turn):
        pairs = [
            (place(2 * line + core, turn ^ (2 * part)), place(2 * line + part, 1 + core))
            for line in range(lines)
            for core in range(2)
            for part in range(2)
        ]
        return lax.ppermute(array, BOTH, pairs)

    def from_workers(array, turn):
        route = [
            (place(2 * line + part, 1 + core), place(2 * line + core, turn ^ (2 * part)))
            for line in range(lines)
            for core in range(2)
            for part in range(2)
        ]
        return lax.ppermute(array, BOTH, route)

    levels = [(lambda t, z: (t ^ 1, z), half), (lambda t, z: (t, 3 - z), upper)]
    distance = 2
    while distance < tm_count:
        levels.append((functools.partial(lambda d, t, z: (t ^ d, z), distance), (tm // distance) % 2))
        distance *= 2

    def swap(array, level, cores=(0, 1)):
        route = [
            (place(t, z), place(*levels[level][0](t, z)))
            for t in range(tm_count)
            for z in (1, 2)
            if t % 2 in cores
        ]
        return lax.ppermute(array, BOTH, route)

    seen_other = lax.ppermute(observations, "tm", [(t, t ^ 1) for t in range(tm_count)])
    gain_shares = [share([filter_gains], latter) for latter in (False, True)]
    gain_parts = [to_workers(gain_shares[turn // 2], turn) for turn in range(4)]
    cov_shares = [share([filt_cov], latter) for latter in (False, True)]
    cov_parts = [to_workers(cov_shares[turn // 2], turn) for turn in range(4)]
    late_shares = [share([smooth_gains], latter) for latter in (False, True)]
    seen = jnp.where(half == upper, observations, seen_other)
    seen = lax.dynamic_slice_in_dim(seen, half * steps, steps, 0)

    trans_map = dynamics * expand_mask(dynamics_mask, width, width)
    obs_map = obs_op * expand_mask(obs_mask, obs_width, width)
    obs_dyn = jnp.matmul(obs_map, trans_map, precision=highest)
    initial = initial_expectation[None, :]
    noise = process_noise[None, :]

    packed_filter = (width + PAD, width)
    packed_smooth = (2 * width + PAD, width)
    stack = (steps, width, width)
    short = (steps, width)

    chunk, maps, shifts = call(filter_chunk, [packed_filter, stack, short], far=[-2, -1])(
        [half], *gain_parts, seen, trans_map.T, obs_dyn.T, *late_shares
    )
    total, arrived, others = chunk, swap(chunk, 0, (1,)), []
    for level in range(len(levels) - 1):
        after = (cov_parts[:2], cov_parts)[level] if level < 2 else []
        after = after + [maps]
        if level == len(levels) - 2:
            after = after + [pred]
        total, state = call(
            filter_join, [packed_filter, (PAD, width)], far=range(-len(after), 0)
        )([levels[level][1] if level else 0], total, arrived, initial, *after)
        if level == 1:
            filt, pred = call(predict, [stack] * 2, far=[-1])(
                [half], *cov_parts, trans_map, noise, state
            )
        if level:
            others.insert(0, (levels[level][1], arrived))
        else:
            *late_shares, total = lax.optimization_barrier((*late_shares, total))
            smooth_parts = [to_workers(late_shares[turn // 2], turn) for turn in range(4)]
        if level < len(levels) - 2:
            arrived = swap(total, level + 1, (0,))
    reached, onward = call(filter_reach, [(PAD, width)] * 2)(
        [levels[-1][1]] + [late for late, _ in others],
        swap(state, len(levels) - 1, (0,)),
        initial,
        chunk,
        *[arrived for _, arrived in others],
    )
    (means,) = call(filter_last, [short])(
        [half], reached, swap(onward, 0, (0,)), maps, shifts
    )

    final = jnp.logical_and(tm // 2 == lines - 1, jnp.logical_and(half == 1, blk == 2))
    plain = (2 * width, width)
    first, maps, covs = call(smooth_chunk, [plain, stack, stack], alias=[(5, 1), (4, 2)], far=[-1])(
        [half, final], *smooth_parts, filt, pred, reached
    )
    offsets, delta = call(smooth_offsets, [short, (PAD, width)])(
        [half, final], *smooth_parts, means, trans_map, maps
    )
    next_cov = swap(first, 0, (1,))
    (total,) = call(smooth_join_cov, [plain], far=[-1])([0], first, next_cov, delta)
    next_delta = swap(delta, 0, (1,))
    (delta,) = call(smooth_join_delta, [(PAD, width)])([0], first, delta, next_delta)
    behind = None
    for level in range(1, len(levels) - 1):
        arrived = swap(total, level, (0,))
        if behind is None:
            arrived = jnp.concatenate([arrived, swap(delta, level, (0,))], axis=0)
            total = jnp.concatenate([total, delta], axis=0)
        late = levels[level][1]
        (total,) = call(smooth_join, [packed_smooth])([late], total, arrived)
        if behind is None:
            behind = jnp.where(late == 0, arrived, jnp.eye(*packed_smooth, dtype=jnp.float32))
        else:
            (behind,) = call(smooth_behind, [packed_smooth])([late], arrived, behind)
    next_total = jnp.concatenate([next_cov, next_delta], axis=0)
    arrived = swap(total[width:], len(levels) - 1, (0,))
    (reached,) = call(smooth_reach, [packed_filter])([levels[-1][1]], arrived, behind)
    piece = (steps * row_count + steps, width)
    pieces = call(smooth_last, [piece] * 4, [packed_filter])(
        [half], reached, swap(reached, 0, (0,)), next_total, maps, covs, offsets
    )
    arrived = [from_workers(pieces[turn], turn) for turn in range(4)]

    mean_out, cov_out = call(
        place_halves,
        [(step_count, row_count), (step_count * row_count, width)],
        [(step_count, width)],
        sems=(2, CUTS + 1),
        far=range(4),
        far_outs=[1],
    )([blk], *arrived)
    return mean_out, cov_out.reshape(step_count, row_count, width)


def solution(mesh):
    return jax.shard_map(
        per_device,
        mesh=mesh,
        in_specs=(
            P(),
            P(),
            P(),
            P(),
            P(),
            P(),
            P("tm", "blk", None),
            P("tm", None),
            P("tm", "blk", None),
            P("tm", "blk", None),
        ),
        out_specs=(P("tm", "blk"), P("tm", "blk", None)),
        check_vma=False,
    )
```

```python
import functools
import math

import jax
import jax.numpy as jnp
from jax import lax
from jax.experimental import pallas as pl
from jax.experimental.pallas import tpu as pltpu
from jax.sharding import PartitionSpec as P

highest = lax.Precision.HIGHEST
BOTH = ("tm", "blk")
PAD = 16
CUTS = 4
SPARE = 4 * 1024 * 1024


def halves(x):
    top = x.astype(jnp.bfloat16)
    return top, (x - top.astype(jnp.float32)).astype(jnp.bfloat16)


def product(left, right, dims):
    def one(a, b):
        return lax.dot_general(a, b, (dims, ((), ())), preferred_element_type=jnp.float32)

    rows = left[0].shape[0]
    both = one(jnp.concatenate(left, axis=0), right[0])
    return both[:rows] + (both[rows:] + one(left[0], right[1]))


def mm(left, right):
    return product(halves(left), halves(right), ((1,), (0,)))


def mm_nt(left, right):
    return product(halves(left), halves(right), ((1,), (1,)))


def under(above, below):
    return tuple(jnp.concatenate([a, b], axis=0) for a, b in zip(above, below))


def rows_of(vec):
    return jnp.broadcast_to(vec, (PAD, vec.shape[-1]))


def expand_mask(mask, row_total, col_total):
    row_block = row_total // mask.shape[0]
    col_block = col_total // mask.shape[1]
    return jnp.repeat(jnp.repeat(mask.astype(jnp.float32), row_block, axis=0), col_block, axis=1)


def whole(pieces, step, half, latter=0):
    parts = [piece[step + latter * (piece.shape[0] - pieces[0].shape[0])] for piece in pieces]
    straight = jnp.concatenate(parts, axis=0)
    return jnp.where(half == 0, straight, jnp.concatenate(parts[2:] + parts[:2], axis=0))


def filter_chunk(where, k0, k1, k2, k3, seen, trans_t, dyn_t, *rest):
    packed, maps, shifts = rest[-3:]
    width = trans_t.shape[0]
    steps = k0.shape[0]
    dyn_parts = halves(dyn_t[...])
    running = [None, None]
    for step in range(steps // 2):
        for part in range(2):
            spot = step + part * (steps // 2)
            gain = halves(whole((k0, k1, k2, k3), spot, where[0]))
            seen_rows = halves(rows_of(seen[spot : spot + 1, :]))
            turned = product(under(dyn_parts, seen_rows), gain, ((1,), (1,)))
            shift = turned[width:]
            turned = trans_t[...] - turned[:width]
            if step == 0:
                running[part] = (turned, shift)
            else:
                running[part] = filter_follow(*running[part], turned, shift)
            maps[spot] = running[part][0]
            shifts[spot : spot + 1, :] = running[part][1][0:1]
    packed[:width], packed[width:] = filter_follow(*running[0], *running[1])


def filter_follow(early_map, early_shift, late_map, late_shift):
    width = late_map.shape[0]
    moved = product(
        under(halves(early_map), halves(early_shift)), halves(late_map), ((1,), (0,))
    )
    return moved[:width], moved[width:] + late_shift


def filter_join(where, own, other, initial, *rest):
    total, state = rest[-2:]
    width = own.shape[1]

    def follow(early, latter):
        total[:width], total[width:] = filter_follow(
            early[:width], early[width:], latter[:width], latter[width:]
        )

    @pl.when(where[0] == 0)
    def _():
        follow(own, other)

    @pl.when(where[0] != 0)
    def _():
        follow(other, own)

    state[...] = mm(rows_of(initial[...]), total[:width]) + total[width:]


def filter_reach(where, state, initial, own, *rest):
    reached, onward = rest[-2:]
    width = own.shape[1]
    current = jnp.where(where[0] == 0, rows_of(initial[...]), state[...])
    for n, other in enumerate(rest[:-2]):
        moved = mm(current, other[:width]) + other[width:]
        current = jnp.where(where[1 + n] == 0, current, moved)
    reached[...] = current
    onward[...] = mm(current, own[:width]) + own[width:]


def filter_last(where, reached, onward, maps, shifts, means):
    steps = maps.shape[0]
    middle = steps // 2
    incoming = jnp.where(where[0] == 0, reached[...], onward[...])
    between = mm(incoming, maps[middle - 1]) + shifts[middle - 1 : middle, :]
    starts = (halves(incoming), halves(between))
    for step in range(steps):
        moved = product(starts[step // middle], halves(maps[step]), ((1,), (0,)))
        means[step : step + 1, :] = moved[0:1] + shifts[step : step + 1, :]


def predict(where, f0, f1, f2, f3, trans, noise, after, filt, pred):
    width = trans.shape[0]
    steps = f0.shape[0]
    trans_parts = halves(trans[...])
    row_no = lax.broadcasted_iota(jnp.int32, (width, width), 0)
    col_no = lax.broadcasted_iota(jnp.int32, (width, width), 1)
    noise_mat = jnp.where(row_no == col_no, noise[...], 0.0)
    for step in range(steps):
        now = whole((f0, f1, f2, f3), step, where[0])
        filt[step] = now
        moved = halves(product(trans_parts, halves(now), ((1,), (0,))))
        pred[step] = product(moved, trans_parts, ((1,), (1,))) + noise_mat


def smooth_chunk(where, g0, g1, g2, g3, filt, pred, after, packed, maps, covs):
    width = filt.shape[1]
    steps = g0.shape[0]
    middle = steps // 2
    state = [None, None]
    for step in reversed(range(middle)):
        for part in range(2):
            spot = step + part * middle
            gain_now = whole((g0, g1, g2, g3), spot, where[0], 1)
            if spot == steps - 1:
                gain_now = jnp.where(where[1] != 0, 0.0, gain_now)
            gain = halves(gain_now)
            if state[part] is None:
                gap, chain = -pred[spot], gain_now
            else:
                cov, chain = state[part]
                gap = cov - pred[spot]
                chain = product(gain, halves(chain), ((1,), (0,)))
            gap = halves(product(gain, halves(gap), ((1,), (0,))))
            cov = filt[spot] + product(gap, gain, ((1,), (1,)))
            state[part] = (cov, chain)
            maps[spot] = chain
            covs[spot] = cov
    (early_cov, early_chain), (cov, chain) = state
    gain = halves(early_chain)
    packed[:width] = product(gain, halves(chain), ((1,), (0,)))
    moved = halves(product(gain, halves(cov), ((1,), (0,))))
    packed[width:] = early_cov + product(moved, gain, ((1,), (1,)))


def smooth_offsets(where, g0, g1, g2, g3, means, trans, maps, offsets, delta):
    steps = g0.shape[0]
    middle = steps // 2
    moved_means = mm_nt(jnp.concatenate([means[...]] * (PAD // steps), axis=0), trans[...])
    state = [None, None]
    for step in reversed(range(middle)):
        for part in range(2):
            spot = step + part * middle
            gain_now = whole((g0, g1, g2, g3), spot, where[0], 1)
            if spot == steps - 1:
                gain_now = jnp.where(where[1] != 0, 0.0, gain_now)
            gap = -rows_of(moved_means[spot : spot + 1, :])
            if state[part] is not None:
                gap = state[part] + gap
            state[part] = rows_of(means[spot : spot + 1, :]) + mm_nt(gap, gain_now)
            offsets[spot : spot + 1, :] = state[part][0:1]
    delta[...] = state[0] + mm_nt(state[1], maps[0])


def smooth_join_cov(where, own, other, after, total):
    width = own.shape[1]
    gain = halves(own[:width])
    total[:width] = product(gain, halves(other[:width]), ((1,), (0,)))
    moved = halves(product(gain, halves(other[width:]), ((1,), (0,))))
    total[width:] = own[width:] + product(moved, gain, ((1,), (1,)))


def smooth_join_delta(where, own, delta, other, total):
    total[...] = delta[...] + mm_nt(other[...], own[: own.shape[1]])


def carry_parts(gain, early_cov, early_mean, cov, mean):
    width = cov.shape[0]
    moved = halves(product(gain, halves(cov), ((1,), (0,))))
    moved = product(under(moved, halves(mean)), gain, ((1,), (1,)))
    return early_cov + moved[:width], early_mean + moved[width:]


def carry(gain, early, latter):
    width = early.shape[1]
    moved = halves(product(gain, halves(latter[:width]), ((1,), (0,))))
    return early + product(under(moved, halves(latter[width:])), gain, ((1,), (1,)))


def smooth_follow(early, latter, target):
    width = early.shape[1]
    gain = halves(early[:width])
    target[:width] = product(gain, halves(latter[:width]), ((1,), (0,)))
    target[width:] = carry(gain, early[width:], latter[width:])


def smooth_join(where, own, other, total):
    @pl.when(where[0] == 0)
    def _():
        smooth_follow(own, other, total)

    @pl.when(where[0] != 0)
    def _():
        smooth_follow(other, own, total)


def smooth_behind(where, other, after, behind):
    @pl.when(where[0] == 0)
    def _():
        smooth_follow(after, other, behind)

    @pl.when(where[0] != 0)
    def _():
        behind[...] = after[...]


def smooth_join_split(where, own, other, chain, tail):
    width = own.shape[1]

    def follow(early, latter):
        gain = halves(early[:width])
        chain[...] = product(gain, halves(latter[:width]), ((1,), (0,)))
        tail[...] = carry(gain, early[width:], latter[width:])

    @pl.when(where[0] == 0)
    def _():
        follow(own, other)

    @pl.when(where[0] != 0)
    def _():
        follow(other, own)


def smooth_reach(where, t1, t2, t3, c2, c13, after, reached, current):
    width = after.shape[1]
    odd = where[0] != 0

    def step(chain, tail):
        current[...] = carry(halves(chain[...]), tail[...], current[...])

    @pl.when(odd)
    def _():
        current[...] = t2[...]
        step(c13, t3)

    @pl.when(jnp.logical_not(odd))
    def _():
        current[...] = t3[...]
        step(c2, t2)
        step(c13, t1)

    reached[...] = carry(halves(after[:width]), after[width:], current[...])


def smooth_last(where, own, other, next_total, maps, covs, offsets, p0, p1, p2, p3, start):
    width = maps.shape[1]
    steps = maps.shape[0]
    middle = steps // 2
    rows = width // 4
    half = where[0]

    @pl.when(half == 0)
    def _():
        start[...] = carry(halves(next_total[:width]), next_total[width:], own[...])

    @pl.when(half != 0)
    def _():
        start[...] = other[...]

    late = (start[:width], start[width:])
    early = carry_parts(
        halves(maps[middle]), covs[middle], rows_of(offsets[middle : middle + 1, :]), *late
    )
    starts = [(halves(cov), halves(mean)) for cov, mean in (early, late)]
    pieces = (p0, p1, p2, p3)
    mean_rows = [None] * steps
    for step in reversed(range(steps)):
        gain = halves(maps[step])
        begun, begun_mean = starts[step // middle]
        moved = halves(product(gain, begun, ((1,), (0,))))
        moved = product(under(moved, begun_mean), gain, ((1,), (1,)))
        cov = covs[step] + moved[:width]
        mean_rows[step] = moved[width : width + 1] + offsets[step : step + 1, :]
        for turn, piece in enumerate(pieces):
            swapped = turn ^ 2
            piece[step * rows : step * rows + rows] = jnp.where(
                half == 0,
                cov[rows * turn : rows * turn + rows],
                cov[rows * swapped : rows * swapped + rows],
            )
    all_means = jnp.concatenate(mean_rows, axis=0)
    for piece in pieces:
        piece[steps * rows :] = all_means


def share_half(where, *refs):
    share = refs[-1]
    wholes = refs[:-1]
    steps = wholes[0].shape[0] // 2

    @pl.when(where[0] == 0)
    def _():
        for n in range(share.shape[0] // steps):
            share[n * steps : n * steps + steps] = wholes[n][:steps]

    @pl.when(where[0] != 0)
    def _():
        for n in range(share.shape[0] // steps):
            share[n * steps : n * steps + steps] = wholes[n][steps:]


def place_halves(where, a0, a1, a2, a3, mean, cov, seen, sems):
    blk = where[0]
    rows = cov.shape[0] // 2
    short = mean.shape[0] // 2
    wide = mean.shape[1]
    parts = (a0, a1, a2, a3)
    cut = rows // CUTS
    for turn in range(4):

        @pl.when(blk == turn)
        def _(turn=turn):
            copies = []
            for part in range(2):
                source = parts[turn ^ (2 * part)]
                pairs = [(source.at[pl.ds(rows, short)], seen.at[pl.ds(part * short, short)])]
                for n in range(CUTS):
                    spot = pl.ds(part * rows + n * cut, cut)
                    pairs.append((source.at[pl.ds(n * cut, cut)], cov.at[spot]))
                for n, pair in enumerate(pairs):
                    copies.append(pltpu.make_async_copy(*pair, sems.at[part, n]))
                    copies[-1].start()
            for copy in copies:
                copy.wait()
            mean[...] = seen[:, wide * turn : wide * turn + wide]


def call(body, outs, scratch=(), sems=(), far=(), far_outs=(), alias=(), grant=None):
    def space(flag):
        return pl.BlockSpec(memory_space=pl.ANY if flag else pltpu.VMEM)

    def run(where, *operands):
        count = len(operands)
        held = [outs[n] for n in range(len(outs)) if n not in far_outs and n not in [b for _, b in alias]] + list(scratch)
        held += [op.shape for n, op in enumerate(operands) if n not in far and n - count not in far]
        limit = grant or 4 * sum(math.prod(shape) for shape in held) + SPARE
        return pl.pallas_call(
            body,
            out_shape=[jax.ShapeDtypeStruct(shape, jnp.float32) for shape in outs],
            in_specs=[pl.BlockSpec(memory_space=pltpu.SMEM)]
            + [space(n in far or n - count in far) for n in range(count)],
            out_specs=[space(n in far_outs) for n in range(len(outs))],
            scratch_shapes=[pltpu.VMEM(shape, jnp.float32) for shape in scratch]
            + ([pltpu.SemaphoreType.DMA(sems)] if sems else []),
            input_output_aliases={1 + a: b for a, b in alias},
            compiler_params=pltpu.CompilerParams(vmem_limit_bytes=limit),
        )(jnp.stack([jnp.int32(w) for w in where]), *operands)

    return run


def per_device(
    dynamics,
    dynamics_mask,
    obs_op,
    obs_mask,
    process_noise,
    initial_expectation,
    filter_gains,
    observations,
    smooth_gains,
    filt_cov,
):
    width = dynamics.shape[0]
    obs_width = obs_op.shape[0]
    step_count, row_count = filter_gains.shape[:2]
    steps = step_count // 2
    tm, blk = lax.axis_index("tm"), lax.axis_index("blk")
    tm_count, blk_count = lax.axis_size("tm"), lax.axis_size("blk")
    lines = tm_count // 2
    half = tm % 2
    worker = jnp.logical_or(blk == 1, blk == 2)
    upper = jnp.int32(blk == 2)

    def place(t, z):
        return t * blk_count + z

    def share(arrays, latter):
        flip = jnp.int32((blk >= 2) != latter)
        shape = (steps * len(arrays),) + arrays[0].shape[1:]
        return call(share_half, [shape])([flip], *arrays)[0]

    def to_workers(array, turn):
        pairs = [
            (place(2 * line + core, turn ^ (2 * part)), place(2 * line + part, 1 + core))
            for line in range(lines)
            for core in range(2)
            for part in range(2)
        ]
        return lax.ppermute(array, BOTH, pairs)

    def from_workers(array, turn):
        route = [
            (place(2 * line + part, 1 + core), place(2 * line + core, turn ^ (2 * part)))
            for line in range(lines)
            for core in range(2)
            for part in range(2)
        ]
        return lax.ppermute(array, BOTH, route)

    levels = [(lambda t, z: (t ^ 1, z), half), (lambda t, z: (t, 3 - z), upper)]
    distance = 2
    while distance < tm_count:
        levels.append((functools.partial(lambda d, t, z: (t ^ d, z), distance), (tm // distance) % 2))
        distance *= 2

    def swap(array, level, cores=(0, 1)):
        route = [
            (place(t, z), place(*levels[level][0](t, z)))
            for t in range(tm_count)
            for z in (1, 2)
            if t % 2 in cores
        ]
        return lax.ppermute(array, BOTH, route)

    seen_other = lax.ppermute(observations, "tm", [(t, t ^ 1) for t in range(tm_count)])
    gain_shares = [share([filter_gains], latter) for latter in (False, True)]
    gain_parts = [to_workers(gain_shares[turn // 2], turn) for turn in range(4)]
    cov_shares = [share([filt_cov], latter) for latter in (False, True)]
    cov_parts = [to_workers(cov_shares[turn // 2], turn) for turn in range(4)]
    late_shares = [share([smooth_gains], latter) for latter in (False, True)]
    seen = jnp.where(half == upper, observations, seen_other)
    seen = lax.dynamic_slice_in_dim(seen, half * steps, steps, 0)

    trans_map = dynamics * expand_mask(dynamics_mask, width, width)
    obs_map = obs_op * expand_mask(obs_mask, obs_width, width)
    obs_dyn = jnp.matmul(obs_map, trans_map, precision=highest)
    initial = initial_expectation[None, :]
    noise = process_noise[None, :]

    packed_filter = (width + PAD, width)
    packed_smooth = (2 * width + PAD, width)
    stack = (steps, width, width)
    short = (steps, width)

    chunk, maps, shifts = call(filter_chunk, [packed_filter, stack, short], far=[-2, -1])(
        [half], *gain_parts, seen, trans_map.T, obs_dyn.T, *late_shares
    )
    total, arrived, others = chunk, swap(chunk, 0, (1,)), []
    for level in range(len(levels) - 1):
        after = (cov_parts[:2], cov_parts)[level] if level < 2 else []
        after = after + [maps]
        if level == len(levels) - 2:
            after = after + [pred]
        total, state = call(
            filter_join, [packed_filter, (PAD, width)], far=range(-len(after), 0)
        )([levels[level][1] if level else 0], total, arrived, initial, *after)
        if level == 1:
            filt, pred = call(predict, [stack] * 2, far=[-1])(
                [half], *cov_parts, trans_map, noise, state
            )
        if level:
            others.insert(0, (levels[level][1], arrived))
        else:
            *late_shares, total = lax.optimization_barrier((*late_shares, total))
            smooth_parts = [to_workers(late_shares[turn // 2], turn) for turn in range(4)]
        if level < len(levels) - 2:
            arrived = swap(total, level + 1, (0,))
    reached, onward = call(filter_reach, [(PAD, width)] * 2)(
        [levels[-1][1]] + [late for late, _ in others],
        swap(state, len(levels) - 1, (0,)),
        initial,
        chunk,
        *[arrived for _, arrived in others],
    )
    (means,) = call(filter_last, [short])(
        [half], reached, swap(onward, 0, (0,)), maps, shifts
    )

    final = jnp.logical_and(tm // 2 == lines - 1, jnp.logical_and(half == 1, blk == 2))
    plain = (2 * width, width)
    first, maps, covs = call(smooth_chunk, [plain, stack, stack], alias=[(5, 1), (4, 2)], far=[-1])(
        [half, final], *smooth_parts, filt, pred, reached
    )
    offsets, delta = call(smooth_offsets, [short, (PAD, width)])(
        [half, final], *smooth_parts, means, trans_map, maps
    )
    next_cov = swap(first, 0, (1,))
    (total,) = call(smooth_join_cov, [plain], far=[-1])([0], first, next_cov, delta)
    next_delta = swap(delta, 0, (1,))
    (delta,) = call(smooth_join_delta, [(PAD, width)])([0], first, delta, next_delta)
    behind = None
    for level in range(1, len(levels) - 2):
        arrived = swap(total, level, (0,))
        if behind is None:
            arrived = jnp.concatenate([arrived, swap(delta, level, (0,))], axis=0)
            total = jnp.concatenate([total, delta], axis=0)
        late = levels[level][1]
        if level == len(levels) - 3:
            chain, tail = call(smooth_join_split, [(width, width), packed_filter])(
                [late], total, arrived
            )
        else:
            (total,) = call(smooth_join, [packed_smooth])([late], total, arrived)
        if behind is None:
            behind = jnp.where(late == 0, arrived, jnp.eye(*packed_smooth, dtype=jnp.float32))
        else:
            (behind,) = call(smooth_behind, [packed_smooth])([late], arrived, behind)
    next_total = jnp.concatenate([next_cov, next_delta], axis=0)
    quarter = tm_count // 4

    def from_later(array, hops):
        pairs = [
            (place(t, z), place(t - (source - target) * quarter, z))
            for t in range(0, tm_count, 2)
            for z in (1, 2)
            for source, target in hops
            if t // quarter == source
        ]
        return lax.ppermute(array, BOTH, pairs)

    tail3 = from_later(tail, ((3, 0), (2, 1)))
    tail2 = from_later(tail, ((3, 1), (2, 0)))
    chain2 = from_later(chain, ((2, 0),))
    chain13 = from_later(chain, ((2, 1), (1, 0)))
    tail1 = from_later(tail, ((3, 2), (1, 0)))
    (reached,) = call(smooth_reach, [packed_filter], [packed_filter])(
        [(tm // quarter) % 2], tail1, tail2, tail3, chain2, chain13, behind
    )
    piece = (steps * row_count + steps, width)
    pieces = call(smooth_last, [piece] * 4, [packed_filter])(
        [half], reached, swap(reached, 0, (0,)), next_total, maps, covs, offsets
    )
    arrived = [from_workers(pieces[turn], turn) for turn in range(4)]

    mean_out, cov_out = call(
        place_halves,
        [(step_count, row_count), (step_count * row_count, width)],
        [(step_count, width)],
        sems=(2, CUTS + 1),
        far=range(4),
        far_outs=[1],
    )([blk], *arrived)
    return mean_out, cov_out.reshape(step_count, row_count, width)


def solution(mesh):
    return jax.shard_map(
        per_device,
        mesh=mesh,
        in_specs=(
            P(),
            P(),
            P(),
            P(),
            P(),
            P(),
            P("tm", "blk", None),
            P("tm", None),
            P("tm", "blk", None),
            P("tm", "blk", None),
        ),
        out_specs=(P("tm", "blk"), P("tm", "blk", None)),
        check_vma=False,
    )
```

```python
import functools
import math

import jax
import jax.numpy as jnp
from jax import lax
from jax.experimental import pallas as pl
from jax.experimental.pallas import tpu as pltpu
from jax.sharding import PartitionSpec as P

highest = lax.Precision.HIGHEST
BOTH = ("tm", "blk")
PAD = 16
CUTS = 4
SPARE = 4 * 1024 * 1024


def halves(x):
    top = x.astype(jnp.bfloat16)
    return top, (x - top.astype(jnp.float32)).astype(jnp.bfloat16)


def product(left, right, dims):
    def one(a, b):
        return lax.dot_general(a, b, (dims, ((), ())), preferred_element_type=jnp.float32)

    rows = left[0].shape[0]
    both = one(jnp.concatenate(left, axis=0), right[0])
    return both[:rows] + (both[rows:] + one(left[0], right[1]))


def mm(left, right):
    return product(halves(left), halves(right), ((1,), (0,)))


def mm_nt(left, right):
    return product(halves(left), halves(right), ((1,), (1,)))


def under(above, below):
    return tuple(jnp.concatenate([a, b], axis=0) for a, b in zip(above, below))


def rows_of(vec):
    return jnp.broadcast_to(vec, (PAD, vec.shape[-1]))


def expand_mask(mask, row_total, col_total):
    row_block = row_total // mask.shape[0]
    col_block = col_total // mask.shape[1]
    return jnp.repeat(jnp.repeat(mask.astype(jnp.float32), row_block, axis=0), col_block, axis=1)


def whole(pieces, step, half, latter=0):
    parts = [piece[step + latter * (piece.shape[0] - pieces[0].shape[0])] for piece in pieces]
    straight = jnp.concatenate(parts, axis=0)
    return jnp.where(half == 0, straight, jnp.concatenate(parts[2:] + parts[:2], axis=0))


def filter_chunk(where, k0, k1, k2, k3, seen, trans_t, dyn_t, *rest):
    packed, maps, shifts = rest[-3:]
    width = trans_t.shape[0]
    steps = k0.shape[0]
    dyn_parts = halves(dyn_t[...])
    running = [None, None]
    for step in range(steps // 2):
        for part in range(2):
            spot = step + part * (steps // 2)
            gain = halves(whole((k0, k1, k2, k3), spot, where[0]))
            seen_rows = halves(rows_of(seen[spot : spot + 1, :]))
            turned = product(under(dyn_parts, seen_rows), gain, ((1,), (1,)))
            shift = turned[width:]
            turned = trans_t[...] - turned[:width]
            if step == 0:
                running[part] = (turned, shift)
            else:
                running[part] = filter_follow(*running[part], turned, shift)
            maps[spot] = running[part][0]
            shifts[spot : spot + 1, :] = running[part][1][0:1]
    packed[:width], packed[width:] = filter_follow(*running[0], *running[1])


def filter_follow(early_map, early_shift, late_map, late_shift):
    width = late_map.shape[0]
    moved = product(
        under(halves(early_map), halves(early_shift)), halves(late_map), ((1,), (0,))
    )
    return moved[:width], moved[width:] + late_shift


def filter_join(where, own, other, *rest):
    total = rest[-1]
    width = own.shape[1]

    def follow(early, latter):
        total[:width], total[width:] = filter_follow(
            early[:width], early[width:], latter[:width], latter[width:]
        )

    @pl.when(where[0] == 0)
    def _():
        follow(own, other)

    @pl.when(where[0] != 0)
    def _():
        follow(other, own)


def filter_ahead(where, own, other, initial, *rest):
    state = rest[-1]
    width = own.shape[1]

    def follow(early, latter):
        moved = mm(rows_of(initial[...]), early[:width]) + early[width:]
        state[...] = mm(moved, latter[:width]) + latter[width:]

    @pl.when(where[0] == 0)
    def _():
        follow(own, other)

    @pl.when(where[0] != 0)
    def _():
        follow(other, own)


def filter_reach(where, state, initial, own, *rest):
    reached, onward = rest[-2:]
    width = own.shape[1]
    current = jnp.where(where[0] == 0, rows_of(initial[...]), state[...])
    for n, other in enumerate(rest[:-2]):
        moved = mm(current, other[:width]) + other[width:]
        current = jnp.where(where[1 + n] == 0, current, moved)
    reached[...] = current
    onward[...] = mm(current, own[:width]) + own[width:]


def filter_last(where, reached, onward, maps, shifts, means):
    steps = maps.shape[0]
    middle = steps // 2
    incoming = jnp.where(where[0] == 0, reached[...], onward[...])
    between = mm(incoming, maps[middle - 1]) + shifts[middle - 1 : middle, :]
    starts = (halves(incoming), halves(between))
    for step in range(steps):
        moved = product(starts[step // middle], halves(maps[step]), ((1,), (0,)))
        means[step : step + 1, :] = moved[0:1] + shifts[step : step + 1, :]


def predict(where, f0, f1, f2, f3, trans, noise, after, filt, pred):
    width = trans.shape[0]
    steps = f0.shape[0]
    trans_parts = halves(trans[...])
    row_no = lax.broadcasted_iota(jnp.int32, (width, width), 0)
    col_no = lax.broadcasted_iota(jnp.int32, (width, width), 1)
    noise_mat = jnp.where(row_no == col_no, noise[...], 0.0)
    for step in range(steps):
        now = whole((f0, f1, f2, f3), step, where[0])
        filt[step] = now
        moved = halves(product(trans_parts, halves(now), ((1,), (0,))))
        pred[step] = product(moved, trans_parts, ((1,), (1,))) + noise_mat


def smooth_chunk(where, g0, g1, g2, g3, filt, pred, after, packed, maps, covs):
    width = filt.shape[1]
    steps = g0.shape[0]
    middle = steps // 2
    state = [None, None]
    for step in reversed(range(middle)):
        for part in range(2):
            spot = step + part * middle
            gain_now = whole((g0, g1, g2, g3), spot, where[0], 1)
            if spot == steps - 1:
                gain_now = jnp.where(where[1] != 0, 0.0, gain_now)
            gain = halves(gain_now)
            if state[part] is None:
                gap, chain = -pred[spot], gain_now
            else:
                cov, chain = state[part]
                gap = cov - pred[spot]
                chain = product(gain, halves(chain), ((1,), (0,)))
            gap = halves(product(gain, halves(gap), ((1,), (0,))))
            cov = filt[spot] + product(gap, gain, ((1,), (1,)))
            state[part] = (cov, chain)
            maps[spot] = chain
            covs[spot] = cov
    (early_cov, early_chain), (cov, chain) = state
    gain = halves(early_chain)
    packed[:width] = product(gain, halves(chain), ((1,), (0,)))
    moved = halves(product(gain, halves(cov), ((1,), (0,))))
    packed[width:] = early_cov + product(moved, gain, ((1,), (1,)))


def smooth_offsets(where, g0, g1, g2, g3, means, trans, maps, offsets, delta):
    steps = g0.shape[0]
    middle = steps // 2
    moved_means = mm_nt(jnp.concatenate([means[...]] * (PAD // steps), axis=0), trans[...])
    state = [None, None]
    for step in reversed(range(middle)):
        for part in range(2):
            spot = step + part * middle
            gain_now = whole((g0, g1, g2, g3), spot, where[0], 1)
            if spot == steps - 1:
                gain_now = jnp.where(where[1] != 0, 0.0, gain_now)
            gap = -rows_of(moved_means[spot : spot + 1, :])
            if state[part] is not None:
                gap = state[part] + gap
            state[part] = rows_of(means[spot : spot + 1, :]) + mm_nt(gap, gain_now)
            offsets[spot : spot + 1, :] = state[part][0:1]
    delta[...] = state[0] + mm_nt(state[1], maps[0])


def smooth_join_cov(where, own, other, after, total):
    width = own.shape[1]
    gain = halves(own[:width])
    total[:width] = product(gain, halves(other[:width]), ((1,), (0,)))
    moved = halves(product(gain, halves(other[width:]), ((1,), (0,))))
    total[width:] = own[width:] + product(moved, gain, ((1,), (1,)))


def smooth_join_delta(where, own, delta, other, total):
    total[...] = delta[...] + mm_nt(other[...], own[: own.shape[1]])


def carry_parts(gain, early_cov, early_mean, cov, mean):
    width = cov.shape[0]
    moved = halves(product(gain, halves(cov), ((1,), (0,))))
    moved = product(under(moved, halves(mean)), gain, ((1,), (1,)))
    return early_cov + moved[:width], early_mean + moved[width:]


def carry(gain, early, latter):
    width = early.shape[1]
    moved = halves(product(gain, halves(latter[:width]), ((1,), (0,))))
    return early + product(under(moved, halves(latter[width:])), gain, ((1,), (1,)))


def smooth_follow(early, latter, target):
    width = early.shape[1]
    gain = halves(early[:width])
    target[:width] = product(gain, halves(latter[:width]), ((1,), (0,)))
    target[width:] = carry(gain, early[width:], latter[width:])


def smooth_join(where, own, other, total):
    @pl.when(where[0] == 0)
    def _():
        smooth_follow(own, other, total)

    @pl.when(where[0] != 0)
    def _():
        smooth_follow(other, own, total)


def smooth_behind(where, other, after, behind):
    @pl.when(where[0] == 0)
    def _():
        smooth_follow(after, other, behind)

    @pl.when(where[0] != 0)
    def _():
        behind[...] = after[...]


def smooth_join_split(where, own, other, chain, tail):
    width = own.shape[1]

    def follow(early, latter):
        gain = halves(early[:width])
        chain[...] = product(gain, halves(latter[:width]), ((1,), (0,)))
        tail[...] = carry(gain, early[width:], latter[width:])

    @pl.when(where[0] == 0)
    def _():
        follow(own, other)

    @pl.when(where[0] != 0)
    def _():
        follow(other, own)


def smooth_reach(where, t1, t2, t3, c2, c13, after, reached, current):
    width = after.shape[1]
    odd = where[0] != 0

    def step(chain, tail):
        current[...] = carry(halves(chain[...]), tail[...], current[...])

    @pl.when(odd)
    def _():
        current[...] = t2[...]
        step(c13, t3)

    @pl.when(jnp.logical_not(odd))
    def _():
        current[...] = t3[...]
        step(c2, t2)
        step(c13, t1)

    reached[...] = carry(halves(after[:width]), after[width:], current[...])


def smooth_last(where, own, other, next_total, maps, covs, offsets, p0, p1, p2, p3, start):
    width = maps.shape[1]
    steps = maps.shape[0]
    middle = steps // 2
    rows = width // 4
    half = where[0]

    @pl.when(half == 0)
    def _():
        start[...] = carry(halves(next_total[:width]), next_total[width:], own[...])

    @pl.when(half != 0)
    def _():
        start[...] = other[...]

    late = (start[:width], start[width:])
    early = carry_parts(
        halves(maps[middle]), covs[middle], rows_of(offsets[middle : middle + 1, :]), *late
    )
    starts = [(halves(cov), halves(mean)) for cov, mean in (early, late)]
    pieces = (p0, p1, p2, p3)
    mean_rows = [None] * steps
    for step in reversed(range(steps)):
        gain = halves(maps[step])
        begun, begun_mean = starts[step // middle]
        moved = halves(product(gain, begun, ((1,), (0,))))
        moved = product(under(moved, begun_mean), gain, ((1,), (1,)))
        cov = covs[step] + moved[:width]
        mean_rows[step] = moved[width : width + 1] + offsets[step : step + 1, :]
        for turn, piece in enumerate(pieces):
            swapped = turn ^ 2
            piece[step * rows : step * rows + rows] = jnp.where(
                half == 0,
                cov[rows * turn : rows * turn + rows],
                cov[rows * swapped : rows * swapped + rows],
            )
    all_means = jnp.concatenate(mean_rows, axis=0)
    for piece in pieces:
        piece[steps * rows :] = all_means


def share_half(where, *refs):
    share = refs[-1]
    wholes = refs[:-1]
    steps = wholes[0].shape[0] // 2

    @pl.when(where[0] == 0)
    def _():
        for n in range(share.shape[0] // steps):
            share[n * steps : n * steps + steps] = wholes[n][:steps]

    @pl.when(where[0] != 0)
    def _():
        for n in range(share.shape[0] // steps):
            share[n * steps : n * steps + steps] = wholes[n][steps:]


def place_halves(where, a0, a1, a2, a3, mean, cov, seen, sems):
    blk = where[0]
    rows = cov.shape[0] // 2
    short = mean.shape[0] // 2
    wide = mean.shape[1]
    parts = (a0, a1, a2, a3)
    cut = rows // CUTS
    for turn in range(4):

        @pl.when(blk == turn)
        def _(turn=turn):
            copies = []
            for part in range(2):
                source = parts[turn ^ (2 * part)]
                pairs = [(source.at[pl.ds(rows, short)], seen.at[pl.ds(part * short, short)])]
                for n in range(CUTS):
                    spot = pl.ds(part * rows + n * cut, cut)
                    pairs.append((source.at[pl.ds(n * cut, cut)], cov.at[spot]))
                for n, pair in enumerate(pairs):
                    copies.append(pltpu.make_async_copy(*pair, sems.at[part, n]))
                    copies[-1].start()
            for copy in copies:
                copy.wait()
            mean[...] = seen[:, wide * turn : wide * turn + wide]


def call(body, outs, scratch=(), sems=(), far=(), far_outs=(), alias=(), grant=None):
    def space(flag):
        return pl.BlockSpec(memory_space=pl.ANY if flag else pltpu.VMEM)

    def run(where, *operands):
        count = len(operands)
        held = [outs[n] for n in range(len(outs)) if n not in far_outs and n not in [b for _, b in alias]] + list(scratch)
        held += [op.shape for n, op in enumerate(operands) if n not in far and n - count not in far]
        limit = grant or 4 * sum(math.prod(shape) for shape in held) + SPARE
        return pl.pallas_call(
            body,
            out_shape=[jax.ShapeDtypeStruct(shape, jnp.float32) for shape in outs],
            in_specs=[pl.BlockSpec(memory_space=pltpu.SMEM)]
            + [space(n in far or n - count in far) for n in range(count)],
            out_specs=[space(n in far_outs) for n in range(len(outs))],
            scratch_shapes=[pltpu.VMEM(shape, jnp.float32) for shape in scratch]
            + ([pltpu.SemaphoreType.DMA(sems)] if sems else []),
            input_output_aliases={1 + a: b for a, b in alias},
            compiler_params=pltpu.CompilerParams(vmem_limit_bytes=limit),
        )(jnp.stack([jnp.int32(w) for w in where]), *operands)

    return run


def per_device(
    dynamics,
    dynamics_mask,
    obs_op,
    obs_mask,
    process_noise,
    initial_expectation,
    filter_gains,
    observations,
    smooth_gains,
    filt_cov,
):
    width = dynamics.shape[0]
    obs_width = obs_op.shape[0]
    step_count, row_count = filter_gains.shape[:2]
    steps = step_count // 2
    tm, blk = lax.axis_index("tm"), lax.axis_index("blk")
    tm_count, blk_count = lax.axis_size("tm"), lax.axis_size("blk")
    lines = tm_count // 2
    half = tm % 2
    worker = jnp.logical_or(blk == 1, blk == 2)
    upper = jnp.int32(blk == 2)

    def place(t, z):
        return t * blk_count + z

    def share(arrays, latter):
        flip = jnp.int32((blk >= 2) != latter)
        shape = (steps * len(arrays),) + arrays[0].shape[1:]
        return call(share_half, [shape])([flip], *arrays)[0]

    def to_workers(array, turn):
        pairs = [
            (place(2 * line + core, turn ^ (2 * part)), place(2 * line + part, 1 + core))
            for line in range(lines)
            for core in range(2)
            for part in range(2)
        ]
        return lax.ppermute(array, BOTH, pairs)

    def from_workers(array, turn):
        route = [
            (place(2 * line + part, 1 + core), place(2 * line + core, turn ^ (2 * part)))
            for line in range(lines)
            for core in range(2)
            for part in range(2)
        ]
        return lax.ppermute(array, BOTH, route)

    levels = [(lambda t, z: (t ^ 1, z), half), (lambda t, z: (t, 3 - z), upper)]
    distance = 2
    while distance < tm_count:
        levels.append((functools.partial(lambda d, t, z: (t ^ d, z), distance), (tm // distance) % 2))
        distance *= 2

    def swap(array, level, cores=(0, 1)):
        route = [
            (place(t, z), place(*levels[level][0](t, z)))
            for t in range(tm_count)
            for z in (1, 2)
            if t % 2 in cores
        ]
        return lax.ppermute(array, BOTH, route)

    seen_other = lax.ppermute(observations, "tm", [(t, t ^ 1) for t in range(tm_count)])
    gain_shares = [share([filter_gains], latter) for latter in (False, True)]
    gain_parts = [to_workers(gain_shares[turn // 2], turn) for turn in range(4)]
    cov_shares = [share([filt_cov], latter) for latter in (False, True)]
    cov_parts = [to_workers(cov_shares[turn // 2], turn) for turn in range(4)]
    late_shares = [share([smooth_gains], latter) for latter in (False, True)]
    seen = jnp.where(half == upper, observations, seen_other)
    seen = lax.dynamic_slice_in_dim(seen, half * steps, steps, 0)

    trans_map = dynamics * expand_mask(dynamics_mask, width, width)
    obs_map = obs_op * expand_mask(obs_mask, obs_width, width)
    obs_dyn = jnp.matmul(obs_map, trans_map, precision=highest)
    initial = initial_expectation[None, :]
    noise = process_noise[None, :]

    packed_filter = (width + PAD, width)
    packed_smooth = (2 * width + PAD, width)
    stack = (steps, width, width)
    short = (steps, width)

    chunk, maps, shifts = call(filter_chunk, [packed_filter, stack, short], far=[-2, -1])(
        [half], *gain_parts, seen, trans_map.T, obs_dyn.T, *late_shares
    )
    total, arrived, others = chunk, swap(chunk, 0, (1,)), []
    for level in range(len(levels) - 1):
        after = (cov_parts[:1], cov_parts)[level] if level < 2 else []
        after = after + [maps]
        if level == len(levels) - 2:
            after = after + [pred]
        operands = ([levels[level][1] if level else 0], total, arrived)
        far = range(-len(after), 0)
        if level == len(levels) - 2:
            (state,) = call(filter_ahead, [(PAD, width)], far=far)(*operands, initial, *after)
        else:
            (total,) = call(filter_join, [packed_filter], far=far)(*operands, *after)
        if level == 1:
            filt, pred = call(predict, [stack] * 2, far=[-1])(
                [half], *cov_parts, trans_map, noise, total
            )
        if level:
            others.insert(0, (levels[level][1], arrived))
        else:
            *late_shares, total = lax.optimization_barrier((*late_shares, total))
            smooth_parts = [to_workers(late_shares[turn // 2], turn) for turn in range(4)]
        if level < len(levels) - 2:
            arrived = swap(total, level + 1, (0,))
    reached, onward = call(filter_reach, [(PAD, width)] * 2)(
        [levels[-1][1]] + [late for late, _ in others],
        swap(state, len(levels) - 1, (0,)),
        initial,
        chunk,
        *[arrived for _, arrived in others],
    )
    (means,) = call(filter_last, [short])(
        [half], reached, swap(onward, 0, (0,)), maps, shifts
    )

    final = jnp.logical_and(tm // 2 == lines - 1, jnp.logical_and(half == 1, blk == 2))
    plain = (2 * width, width)
    first, maps, covs = call(smooth_chunk, [plain, stack, stack], alias=[(5, 1), (4, 2)], far=[-1])(
        [half, final], *smooth_parts, filt, pred, reached
    )
    offsets, delta = call(smooth_offsets, [short, (PAD, width)])(
        [half, final], *smooth_parts, means, trans_map, maps
    )
    next_cov = swap(first, 0, (1,))
    (total,) = call(smooth_join_cov, [plain], far=[-1])([0], first, next_cov, delta)
    next_delta = swap(delta, 0, (1,))
    (delta,) = call(smooth_join_delta, [(PAD, width)])([0], first, delta, next_delta)
    behind = None
    for level in range(1, len(levels) - 2):
        arrived = swap(total, level, (0,))
        if behind is None:
            arrived = jnp.concatenate([arrived, swap(delta, level, (0,))], axis=0)
            total = jnp.concatenate([total, delta], axis=0)
        late = levels[level][1]
        if level == len(levels) - 3:
            chain, tail = call(smooth_join_split, [(width, width), packed_filter])(
                [late], total, arrived
            )
        else:
            (total,) = call(smooth_join, [packed_smooth])([late], total, arrived)
        if behind is None:
            behind = jnp.where(late == 0, arrived, jnp.eye(*packed_smooth, dtype=jnp.float32))
        else:
            (behind,) = call(smooth_behind, [packed_smooth])([late], arrived, behind)
    next_total = jnp.concatenate([next_cov, next_delta], axis=0)
    quarter = tm_count // 4

    def from_later(array, hops):
        pairs = [
            (place(t, z), place(t - (source - target) * quarter, z))
            for t in range(0, tm_count, 2)
            for z in (1, 2)
            for source, target in hops
            if t // quarter == source
        ]
        return lax.ppermute(array, BOTH, pairs)

    tail3 = from_later(tail, ((3, 0), (2, 1)))
    tail2 = from_later(tail, ((3, 1), (2, 0)))
    chain2 = from_later(chain, ((2, 0),))
    chain13 = from_later(chain, ((2, 1), (1, 0)))
    tail1 = from_later(tail, ((3, 2), (1, 0)))
    (reached,) = call(smooth_reach, [packed_filter], [packed_filter])(
        [(tm // quarter) % 2], tail1, tail2, tail3, chain2, chain13, behind
    )
    piece = (steps * row_count + steps, width)
    pieces = call(smooth_last, [piece] * 4, [packed_filter])(
        [half], reached, swap(reached, 0, (0,)), next_total, maps, covs, offsets
    )
    arrived = [from_workers(pieces[turn], turn) for turn in range(4)]

    mean_out, cov_out = call(
        place_halves,
        [(step_count, row_count), (step_count * row_count, width)],
        [(step_count, width)],
        sems=(2, CUTS + 1),
        far=range(4),
        far_outs=[1],
    )([blk], *arrived)
    return mean_out, cov_out.reshape(step_count, row_count, width)


def solution(mesh):
    return jax.shard_map(
        per_device,
        mesh=mesh,
        in_specs=(
            P(),
            P(),
            P(),
            P(),
            P(),
            P(),
            P("tm", "blk", None),
            P("tm", None),
            P("tm", "blk", None),
            P("tm", "blk", None),
        ),
        out_specs=(P("tm", "blk"), P("tm", "blk", None)),
        check_vma=False,
    )
```

```python
import functools
import math

import jax
import jax.numpy as jnp
from jax import lax
from jax.experimental import pallas as pl
from jax.experimental.pallas import tpu as pltpu
from jax.sharding import PartitionSpec as P

highest = lax.Precision.HIGHEST
BOTH = ("tm", "blk")
PAD = 16
CUTS = 8
SPARE = 4 * 1024 * 1024


def halves(x):
    top = x.astype(jnp.bfloat16)
    return top, (x - top.astype(jnp.float32)).astype(jnp.bfloat16)


def product(left, right, dims):
    def one(a, b):
        return lax.dot_general(a, b, (dims, ((), ())), preferred_element_type=jnp.float32)

    rows = left[0].shape[0]
    both = one(jnp.concatenate(left, axis=0), right[0])
    return both[:rows] + (both[rows:] + one(left[0], right[1]))


def mm(left, right):
    return product(halves(left), halves(right), ((1,), (0,)))


def mm_nt(left, right):
    return product(halves(left), halves(right), ((1,), (1,)))


def under(above, below):
    return tuple(jnp.concatenate([a, b], axis=0) for a, b in zip(above, below))


def rows_of(vec):
    return jnp.broadcast_to(vec, (PAD, vec.shape[-1]))


def expand_mask(mask, row_total, col_total):
    row_block = row_total // mask.shape[0]
    col_block = col_total // mask.shape[1]
    return jnp.repeat(jnp.repeat(mask.astype(jnp.float32), row_block, axis=0), col_block, axis=1)


def whole(pieces, step, half, latter=0):
    parts = [piece[step + latter * (piece.shape[0] - pieces[0].shape[0])] for piece in pieces]
    straight = jnp.concatenate(parts, axis=0)
    return jnp.where(half == 0, straight, jnp.concatenate(parts[2:] + parts[:2], axis=0))


def filter_chunk(where, k0, k1, k2, k3, seen, trans_t, dyn_t, *rest):
    packed, maps, shifts = rest[-3:]
    width = trans_t.shape[0]
    steps = k0.shape[0]
    dyn_parts = halves(dyn_t[...])
    running = [None, None]
    for step in range(steps // 2):
        for part in range(2):
            spot = step + part * (steps // 2)
            gain = halves(whole((k0, k1, k2, k3), spot, where[0]))
            seen_rows = halves(rows_of(seen[spot : spot + 1, :]))
            turned = product(under(dyn_parts, seen_rows), gain, ((1,), (1,)))
            shift = turned[width:]
            turned = trans_t[...] - turned[:width]
            if step == 0:
                running[part] = (turned, shift)
            else:
                running[part] = filter_follow(*running[part], turned, shift)
            maps[spot] = running[part][0]
            shifts[spot : spot + 1, :] = running[part][1][0:1]
    packed[:width], packed[width:] = filter_follow(*running[0], *running[1])


def filter_follow(early_map, early_shift, late_map, late_shift):
    width = late_map.shape[0]
    moved = product(
        under(halves(early_map), halves(early_shift)), halves(late_map), ((1,), (0,))
    )
    return moved[:width], moved[width:] + late_shift


def filter_join(where, own, other, *rest):
    total = rest[-1]
    width = own.shape[1]

    def follow(early, latter):
        total[:width], total[width:] = filter_follow(
            early[:width], early[width:], latter[:width], latter[width:]
        )

    @pl.when(where[0] == 0)
    def _():
        follow(own, other)

    @pl.when(where[0] != 0)
    def _():
        follow(other, own)


def filter_ahead(where, own, other, initial, *rest):
    state = rest[-1]
    width = own.shape[1]

    def follow(early, latter):
        moved = mm(rows_of(initial[...]), early[:width]) + early[width:]
        state[...] = mm(moved, latter[:width]) + latter[width:]

    @pl.when(where[0] == 0)
    def _():
        follow(own, other)

    @pl.when(where[0] != 0)
    def _():
        follow(other, own)


def filter_reach(where, state, initial, own, *rest):
    reached, onward = rest[-2:]
    width = own.shape[1]
    current = jnp.where(where[0] == 0, rows_of(initial[...]), state[...])
    for n, other in enumerate(rest[:-2]):
        moved = mm(current, other[:width]) + other[width:]
        current = jnp.where(where[1 + n] == 0, current, moved)
    reached[...] = current
    onward[...] = mm(current, own[:width]) + own[width:]


def filter_last(where, reached, onward, maps, shifts, means):
    steps = maps.shape[0]
    middle = steps // 2
    incoming = jnp.where(where[0] == 0, reached[...], onward[...])
    between = mm(incoming, maps[middle - 1]) + shifts[middle - 1 : middle, :]
    starts = (halves(incoming), halves(between))
    for step in range(steps):
        moved = product(starts[step // middle], halves(maps[step]), ((1,), (0,)))
        means[step : step + 1, :] = moved[0:1] + shifts[step : step + 1, :]


def predict(where, f0, f1, f2, f3, trans, noise, after, filt, pred):
    width = trans.shape[0]
    steps = f0.shape[0]
    trans_parts = halves(trans[...])
    row_no = lax.broadcasted_iota(jnp.int32, (width, width), 0)
    col_no = lax.broadcasted_iota(jnp.int32, (width, width), 1)
    noise_mat = jnp.where(row_no == col_no, noise[...], 0.0)
    for step in range(steps):
        now = whole((f0, f1, f2, f3), step, where[0])
        filt[step] = now
        moved = halves(product(trans_parts, halves(now), ((1,), (0,))))
        pred[step] = product(moved, trans_parts, ((1,), (1,))) + noise_mat


def smooth_chunk(where, g0, g1, g2, g3, filt, pred, after, packed, maps, covs):
    width = filt.shape[1]
    steps = g0.shape[0]
    middle = steps // 2
    state = [None, None]
    for step in reversed(range(middle)):
        for part in range(2):
            spot = step + part * middle
            gain_now = whole((g0, g1, g2, g3), spot, where[0], 1)
            if spot == steps - 1:
                gain_now = jnp.where(where[1] != 0, 0.0, gain_now)
            gain = halves(gain_now)
            if state[part] is None:
                gap, chain = -pred[spot], gain_now
            else:
                cov, chain = state[part]
                gap = cov - pred[spot]
                chain = product(gain, halves(chain), ((1,), (0,)))
            gap = halves(product(gain, halves(gap), ((1,), (0,))))
            cov = filt[spot] + product(gap, gain, ((1,), (1,)))
            state[part] = (cov, chain)
            maps[spot] = chain
            covs[spot] = cov
    (early_cov, early_chain), (cov, chain) = state
    gain = halves(early_chain)
    packed[:width] = product(gain, halves(chain), ((1,), (0,)))
    moved = halves(product(gain, halves(cov), ((1,), (0,))))
    packed[width:] = early_cov + product(moved, gain, ((1,), (1,)))


def smooth_offsets(where, g0, g1, g2, g3, means, trans, maps, offsets, delta):
    steps = g0.shape[0]
    middle = steps // 2
    moved_means = mm_nt(jnp.concatenate([means[...]] * (PAD // steps), axis=0), trans[...])
    state = [None, None]
    for step in reversed(range(middle)):
        for part in range(2):
            spot = step + part * middle
            gain_now = whole((g0, g1, g2, g3), spot, where[0], 1)
            if spot == steps - 1:
                gain_now = jnp.where(where[1] != 0, 0.0, gain_now)
            gap = -rows_of(moved_means[spot : spot + 1, :])
            if state[part] is not None:
                gap = state[part] + gap
            state[part] = rows_of(means[spot : spot + 1, :]) + mm_nt(gap, gain_now)
            offsets[spot : spot + 1, :] = state[part][0:1]
    delta[...] = state[0] + mm_nt(state[1], maps[0])


def smooth_join_cov(where, own, other, after, total):
    width = own.shape[1]
    gain = halves(own[:width])
    total[:width] = product(gain, halves(other[:width]), ((1,), (0,)))
    moved = halves(product(gain, halves(other[width:]), ((1,), (0,))))
    total[width:] = own[width:] + product(moved, gain, ((1,), (1,)))


def smooth_join_delta(where, own, delta, other, total):
    total[...] = delta[...] + mm_nt(other[...], own[: own.shape[1]])


def carry_parts(gain, early_cov, early_mean, cov, mean):
    width = cov.shape[0]
    moved = halves(product(gain, halves(cov), ((1,), (0,))))
    moved = product(under(moved, halves(mean)), gain, ((1,), (1,)))
    return early_cov + moved[:width], early_mean + moved[width:]


def carry(gain, early, latter):
    width = early.shape[1]
    moved = halves(product(gain, halves(latter[:width]), ((1,), (0,))))
    return early + product(under(moved, halves(latter[width:])), gain, ((1,), (1,)))


def smooth_follow(early, latter, target):
    width = early.shape[1]
    gain = halves(early[:width])
    target[:width] = product(gain, halves(latter[:width]), ((1,), (0,)))
    target[width:] = carry(gain, early[width:], latter[width:])


def smooth_join(where, own, other, total):
    @pl.when(where[0] == 0)
    def _():
        smooth_follow(own, other, total)

    @pl.when(where[0] != 0)
    def _():
        smooth_follow(other, own, total)


def smooth_behind(where, other, after, behind):
    @pl.when(where[0] == 0)
    def _():
        smooth_follow(after, other, behind)

    @pl.when(where[0] != 0)
    def _():
        behind[...] = after[...]


def smooth_join_split(where, own, other, chain, tail):
    width = own.shape[1]

    def follow(early, latter):
        gain = halves(early[:width])
        chain[...] = product(gain, halves(latter[:width]), ((1,), (0,)))
        tail[...] = carry(gain, early[width:], latter[width:])

    @pl.when(where[0] == 0)
    def _():
        follow(own, other)

    @pl.when(where[0] != 0)
    def _():
        follow(other, own)


def smooth_reach(where, t1, t2, t3, c2, c13, after, reached, current):
    width = after.shape[1]
    odd = where[0] != 0

    def step(chain, tail):
        current[...] = carry(halves(chain[...]), tail[...], current[...])

    @pl.when(odd)
    def _():
        current[...] = t2[...]
        step(c13, t3)

    @pl.when(jnp.logical_not(odd))
    def _():
        current[...] = t3[...]
        step(c2, t2)
        step(c13, t1)

    reached[...] = carry(halves(after[:width]), after[width:], current[...])


def smooth_last(where, own, other, next_total, maps, covs, offsets, p0, p1, p2, p3, start):
    width = maps.shape[1]
    steps = maps.shape[0]
    middle = steps // 2
    rows = width // 4
    half = where[0]

    @pl.when(half == 0)
    def _():
        start[...] = carry(halves(next_total[:width]), next_total[width:], own[...])

    @pl.when(half != 0)
    def _():
        start[...] = other[...]

    late = (start[:width], start[width:])
    early = carry_parts(
        halves(maps[middle]), covs[middle], rows_of(offsets[middle : middle + 1, :]), *late
    )
    starts = [(halves(cov), halves(mean)) for cov, mean in (early, late)]
    pieces = (p0, p1, p2, p3)
    mean_rows = [None] * steps
    for step in reversed(range(steps)):
        gain = halves(maps[step])
        begun, begun_mean = starts[step // middle]
        moved = halves(product(gain, begun, ((1,), (0,))))
        moved = product(under(moved, begun_mean), gain, ((1,), (1,)))
        cov = covs[step] + moved[:width]
        mean_rows[step] = moved[width : width + 1] + offsets[step : step + 1, :]
        for turn, piece in enumerate(pieces):
            swapped = turn ^ 2
            piece[step * rows : step * rows + rows] = jnp.where(
                half == 0,
                cov[rows * turn : rows * turn + rows],
                cov[rows * swapped : rows * swapped + rows],
            )
    all_means = jnp.concatenate(mean_rows, axis=0)
    for piece in pieces:
        piece[steps * rows :] = all_means


def share_half(where, *refs):
    share = refs[-1]
    wholes = refs[:-1]
    steps = wholes[0].shape[0] // 2

    @pl.when(where[0] == 0)
    def _():
        for n in range(share.shape[0] // steps):
            share[n * steps : n * steps + steps] = wholes[n][:steps]

    @pl.when(where[0] != 0)
    def _():
        for n in range(share.shape[0] // steps):
            share[n * steps : n * steps + steps] = wholes[n][steps:]


def place_halves(where, a0, a1, a2, a3, mean, cov, seen, sems):
    blk = where[0]
    rows = cov.shape[0] // 2
    short = mean.shape[0] // 2
    wide = mean.shape[1]
    parts = (a0, a1, a2, a3)
    cut = rows // CUTS
    for turn in range(4):

        @pl.when(blk == turn)
        def _(turn=turn):
            copies = []
            for part in range(2):
                source = parts[turn ^ (2 * part)]
                pairs = [(source.at[pl.ds(rows, short)], seen.at[pl.ds(part * short, short)])]
                for n in range(CUTS):
                    spot = pl.ds(part * rows + n * cut, cut)
                    pairs.append((source.at[pl.ds(n * cut, cut)], cov.at[spot]))
                for n, pair in enumerate(pairs):
                    copies.append(pltpu.make_async_copy(*pair, sems.at[part, n]))
                    copies[-1].start()
            for copy in copies:
                copy.wait()
            mean[...] = seen[:, wide * turn : wide * turn + wide]


def call(body, outs, scratch=(), sems=(), far=(), far_outs=(), alias=(), grant=None):
    def space(flag):
        return pl.BlockSpec(memory_space=pl.ANY if flag else pltpu.VMEM)

    def run(where, *operands):
        count = len(operands)
        held = [outs[n] for n in range(len(outs)) if n not in far_outs and n not in [b for _, b in alias]] + list(scratch)
        held += [op.shape for n, op in enumerate(operands) if n not in far and n - count not in far]
        limit = grant or 4 * sum(math.prod(shape) for shape in held) + SPARE
        return pl.pallas_call(
            body,
            out_shape=[jax.ShapeDtypeStruct(shape, jnp.float32) for shape in outs],
            in_specs=[pl.BlockSpec(memory_space=pltpu.SMEM)]
            + [space(n in far or n - count in far) for n in range(count)],
            out_specs=[space(n in far_outs) for n in range(len(outs))],
            scratch_shapes=[pltpu.VMEM(shape, jnp.float32) for shape in scratch]
            + ([pltpu.SemaphoreType.DMA(sems)] if sems else []),
            input_output_aliases={1 + a: b for a, b in alias},
            compiler_params=pltpu.CompilerParams(vmem_limit_bytes=limit),
        )(jnp.stack([jnp.int32(w) for w in where]), *operands)

    return run


def per_device(
    dynamics,
    dynamics_mask,
    obs_op,
    obs_mask,
    process_noise,
    initial_expectation,
    filter_gains,
    observations,
    smooth_gains,
    filt_cov,
):
    width = dynamics.shape[0]
    obs_width = obs_op.shape[0]
    step_count, row_count = filter_gains.shape[:2]
    steps = step_count // 2
    tm, blk = lax.axis_index("tm"), lax.axis_index("blk")
    tm_count, blk_count = lax.axis_size("tm"), lax.axis_size("blk")
    lines = tm_count // 2
    half = tm % 2
    worker = jnp.logical_or(blk == 1, blk == 2)
    upper = jnp.int32(blk == 2)

    def place(t, z):
        return t * blk_count + z

    def share(arrays, latter):
        flip = jnp.int32((blk >= 2) != latter)
        shape = (steps * len(arrays),) + arrays[0].shape[1:]
        return call(share_half, [shape])([flip], *arrays)[0]

    def to_workers(array, turn):
        pairs = [
            (place(2 * line + core, turn ^ (2 * part)), place(2 * line + part, 1 + core))
            for line in range(lines)
            for core in range(2)
            for part in range(2)
        ]
        return lax.ppermute(array, BOTH, pairs)

    def from_workers(array, turn):
        route = [
            (place(2 * line + part, 1 + core), place(2 * line + core, turn ^ (2 * part)))
            for line in range(lines)
            for core in range(2)
            for part in range(2)
        ]
        return lax.ppermute(array, BOTH, route)

    levels = [(lambda t, z: (t ^ 1, z), half), (lambda t, z: (t, 3 - z), upper)]
    distance = 2
    while distance < tm_count:
        levels.append((functools.partial(lambda d, t, z: (t ^ d, z), distance), (tm // distance) % 2))
        distance *= 2

    def swap(array, level, cores=(0, 1)):
        route = [
            (place(t, z), place(*levels[level][0](t, z)))
            for t in range(tm_count)
            for z in (1, 2)
            if t % 2 in cores
        ]
        return lax.ppermute(array, BOTH, route)

    seen_other = lax.ppermute(observations, "tm", [(t, t ^ 1) for t in range(tm_count)])
    gain_shares = [share([filter_gains], latter) for latter in (False, True)]
    gain_parts = [to_workers(gain_shares[turn // 2], turn) for turn in range(4)]
    cov_shares = [share([filt_cov], latter) for latter in (False, True)]
    cov_parts = [to_workers(cov_shares[turn // 2], turn) for turn in range(4)]
    late_shares = [share([smooth_gains], latter) for latter in (False, True)]
    seen = jnp.where(half == upper, observations, seen_other)
    seen = lax.dynamic_slice_in_dim(seen, half * steps, steps, 0)

    trans_map = dynamics * expand_mask(dynamics_mask, width, width)
    obs_map = obs_op * expand_mask(obs_mask, obs_width, width)
    obs_dyn = jnp.matmul(obs_map, trans_map, precision=highest)
    initial = initial_expectation[None, :]
    noise = process_noise[None, :]

    packed_filter = (width + PAD, width)
    packed_smooth = (2 * width + PAD, width)
    stack = (steps, width, width)
    short = (steps, width)

    chunk, maps, shifts = call(filter_chunk, [packed_filter, stack, short], far=[-2, -1])(
        [half], *gain_parts, seen, trans_map.T, obs_dyn.T, *late_shares
    )
    total, arrived, others = chunk, swap(chunk, 0, (1,)), []
    for level in range(len(levels) - 1):
        after = (cov_parts[:1], cov_parts)[level] if level < 2 else []
        after = after + [maps]
        if level == len(levels) - 2:
            after = after + [pred]
        operands = ([levels[level][1] if level else 0], total, arrived)
        far = range(-len(after), 0)
        if level == len(levels) - 2:
            (state,) = call(filter_ahead, [(PAD, width)], far=far)(*operands, initial, *after)
        else:
            (total,) = call(filter_join, [packed_filter], far=far)(*operands, *after)
        if level == 1:
            filt, pred = call(predict, [stack] * 2, far=[-1])(
                [half], *cov_parts, trans_map, noise, total
            )
        if level:
            others.insert(0, (levels[level][1], arrived))
        else:
            *late_shares, total = lax.optimization_barrier((*late_shares, total))
            smooth_parts = [to_workers(late_shares[turn // 2], turn) for turn in range(4)]
        if level < len(levels) - 2:
            arrived = swap(total, level + 1, (0,))
    reached, onward = call(filter_reach, [(PAD, width)] * 2)(
        [levels[-1][1]] + [late for late, _ in others],
        swap(state, len(levels) - 1, (0,)),
        initial,
        chunk,
        *[arrived for _, arrived in others],
    )
    (means,) = call(filter_last, [short])(
        [half], reached, swap(onward, 0, (0,)), maps, shifts
    )

    final = jnp.logical_and(tm // 2 == lines - 1, jnp.logical_and(half == 1, blk == 2))
    plain = (2 * width, width)
    first, maps, covs = call(smooth_chunk, [plain, stack, stack], alias=[(5, 1), (4, 2)], far=[-1])(
        [half, final], *smooth_parts, filt, pred, reached
    )
    offsets, delta = call(smooth_offsets, [short, (PAD, width)])(
        [half, final], *smooth_parts, means, trans_map, maps
    )
    next_cov = swap(first, 0, (1,))
    (total,) = call(smooth_join_cov, [plain], far=[-1])([0], first, next_cov, delta)
    next_delta = swap(delta, 0, (1,))
    (delta,) = call(smooth_join_delta, [(PAD, width)])([0], first, delta, next_delta)
    behind = None
    for level in range(1, len(levels) - 2):
        arrived = swap(total, level, (0,))
        if behind is None:
            arrived = jnp.concatenate([arrived, swap(delta, level, (0,))], axis=0)
            total = jnp.concatenate([total, delta], axis=0)
        late = levels[level][1]
        if level == len(levels) - 3:
            chain, tail = call(smooth_join_split, [(width, width), packed_filter])(
                [late], total, arrived
            )
        else:
            (total,) = call(smooth_join, [packed_smooth])([late], total, arrived)
        if behind is None:
            behind = jnp.where(late == 0, arrived, jnp.eye(*packed_smooth, dtype=jnp.float32))
        else:
            (behind,) = call(smooth_behind, [packed_smooth])([late], arrived, behind)
    next_total = jnp.concatenate([next_cov, next_delta], axis=0)
    quarter = tm_count // 4

    def from_later(array, hops):
        pairs = [
            (place(t, z), place(t - (source - target) * quarter, z))
            for t in range(0, tm_count, 2)
            for z in (1, 2)
            for source, target in hops
            if t // quarter == source
        ]
        return lax.ppermute(array, BOTH, pairs)

    tail3 = from_later(tail, ((3, 0), (2, 1)))
    tail2 = from_later(tail, ((3, 1), (2, 0)))
    chain2 = from_later(chain, ((2, 0),))
    chain13 = from_later(chain, ((2, 1), (1, 0)))
    tail1 = from_later(tail, ((3, 2), (1, 0)))
    (reached,) = call(smooth_reach, [packed_filter], [packed_filter])(
        [(tm // quarter) % 2], tail1, tail2, tail3, chain2, chain13, behind
    )
    piece = (steps * row_count + steps, width)
    pieces = call(smooth_last, [piece] * 4, [packed_filter])(
        [half], reached, swap(reached, 0, (0,)), next_total, maps, covs, offsets
    )
    arrived = [from_workers(pieces[turn], turn) for turn in range(4)]

    mean_out, cov_out = call(
        place_halves,
        [(step_count, row_count), (step_count * row_count, width)],
        [(step_count, width)],
        sems=(2, CUTS + 1),
        far=range(4),
        far_outs=[1],
    )([blk], *arrived)
    return mean_out, cov_out.reshape(step_count, row_count, width)


def solution(mesh):
    return jax.shard_map(
        per_device,
        mesh=mesh,
        in_specs=(
            P(),
            P(),
            P(),
            P(),
            P(),
            P(),
            P("tm", "blk", None),
            P("tm", None),
            P("tm", "blk", None),
            P("tm", "blk", None),
        ),
        out_specs=(P("tm", "blk"), P("tm", "blk", None)),
        check_vma=False,
    )
```
